32 devices in a mesh: dp: 8 (over z, x), blk: 4 (over y, core).
Axes of the slice: x: 2, y: 2, z: 4, core: 2. Of those that a mesh axis runs over, the one named last changes fastest.
Arguments:
- tokens: bfloat16 [1024, 16384], P('dp', 'blk'), may hold values from -6 to 6
- up_first: bfloat16 [128, 128, 128], P('blk', 'dp'), may hold values from -0.5 to 0.5
- up_second: bfloat16 [128, 128, 256], P('blk', 'dp'), may hold values from -0.5 to 0.5
- down_first: bfloat16 [128, 256, 128], P('blk', 'dp'), may hold values from -0.375 to 0.375
- down_second: bfloat16 [128, 128, 128], P('blk', 'dp'), may hold values from -0.5 to 0.5
- cotangent: bfloat16 [1024, 16384], P('dp', 'blk'), may hold values from -6 to 6
Outputs:
- input_grad: bfloat16 [1024, 16384], P('dp', 'blk')
- up_first_grad: float32 [128, 128, 128], P('blk')
- up_second_grad: float32 [128, 128, 256], P('blk', 'dp')
- down_first_grad: float32 [128, 256, 128], P('blk', 'dp')
- down_second_grad: float32 [128, 128, 128], P('blk')
The draws below stay inside these ranges and needn't reach their ends.
All inputs are finite; a program needn't handle non-finite values.
Results may differ from the reference program's by a relative error of at most 0.0069.
Values may be sent and summed in bfloat16 or wider, within the bound.
A program may use at most 128 MiB of HBM per device.

```python
import math
import jax
import jax.numpy as jnp
from jax import lax

NB = 128
BS = 128
HB = 256
TOK_DEV = 128
WIDTH = 16384
TOKENS = 1024


def steps_of(own_key, dims, cuts, least, largest):
    gain = 1.0
    for position, blocks in cuts:
        steps = jax.random.uniform(jax.random.fold_in(jax.random.fold_in(own_key, 6), position), (blocks,), jnp.float32, least / len(cuts), largest / len(cuts))
        gain = gain * jnp.repeat(jnp.exp(steps), dims[position] // blocks).reshape((-1,) + (1,) * (len(dims) - 1 - position))
    return gain


def noise(stream_key, dims, scale, bound, cuts=(), dtype=jnp.bfloat16):
    drawn = scale * jax.random.normal(stream_key, dims, jnp.float32)
    if cuts:
        drawn = drawn * steps_of(stream_key, dims, cuts, -0.22, 0.18)
    return jnp.clip(drawn, -bound, bound).astype(dtype)


def setup_inputs(seed: int = 0) -> dict:
    seeds = jax.random.split(jax.random.key(seed), 7)
    return {
        "tokens": noise(seeds[0], (TOKENS, WIDTH), 1.0, 6.0, ((0, 8), (1, 4))),
        "up_first": noise(seeds[1], (NB, BS, BS), BS ** -0.5, 0.5, ((0, 4), (1, 8))),
        "up_second": noise(seeds[2], (NB, BS, HB), BS ** -0.5, 0.5, ((0, 4), (1, 8))),
        "down_first": noise(seeds[3], (NB, HB, BS), HB ** -0.5, 0.375, ((0, 4), (1, 8))),
        "down_second": noise(seeds[4], (NB, BS, BS), BS ** -0.5, 0.5, ((0, 4), (1, 8))),
        "cotangent": noise(seeds[5], (TOKENS, WIDTH), 1.0, 6.0, ((0, 8), (1, 4))),
    }


def activation(values):
    return jax.nn.gelu(values, approximate=True)

def window_pass(inputs, upstream, up_first, up_second, down_first, down_second):
    rows_here = inputs.shape[0]
    wide = jnp.float32
    inputs_w = inputs.reshape(rows_here, NB, BS).astype(wide)
    upstream_w = upstream.reshape(rows_here, NB, BS).astype(wide)
    first_up = jnp.einsum('tbi,bij->tbj', inputs_w, up_first.astype(wide)).astype(jnp.bfloat16)
    pre_act = jnp.einsum('tbj,jbk->tjk', first_up.astype(wide), up_second.astype(wide))
    hidden = activation(pre_act).astype(jnp.bfloat16)
    hidden_w = hidden.astype(wide)
    first_down = jnp.einsum('tbi,bij->tbj', hidden_w, down_first.astype(wide)).astype(jnp.bfloat16)
    grad_ds = jnp.einsum('tbj,tjk->jbk', first_down.astype(wide), upstream_w)
    back_down = jnp.einsum('tjk,jbk->tbj', upstream_w, down_second.astype(wide)).astype(jnp.bfloat16)
    back_down_w = back_down.astype(wide)
    grad_df = jnp.einsum('tbi,tbj->bij', hidden_w, back_down_w)
    hidden_grad = jnp.einsum('tbj,bij->tbi', back_down_w, down_first.astype(wide))
    _, pull_back = jax.vjp(activation, pre_act)
    pre_grad = pull_back(hidden_grad)[0].astype(jnp.bfloat16)
    pre_grad_w = pre_grad.astype(wide)
    grad_us = jnp.einsum('tbj,tjk->jbk', first_up.astype(wide), pre_grad_w)
    back_up = jnp.einsum('tjk,jbk->tbj', pre_grad_w, up_second.astype(wide)).astype(jnp.bfloat16)
    back_up_w = back_up.astype(wide)
    grad_uf = jnp.einsum('tbi,tbj->bij', inputs_w, back_up_w)
    input_grad = jnp.einsum('tbj,bij->tbi', back_up_w, up_first.astype(wide)).astype(jnp.bfloat16)
    return (input_grad.reshape(rows_here, NB * BS), grad_uf, grad_us, grad_df, grad_ds)

def reference(tokens, up_first, up_second, down_first, down_second, cotangent):
    blocks_in = tokens.reshape(TOKENS // TOK_DEV, TOK_DEV, NB * BS)
    blocks_up = cotangent.reshape(TOKENS // TOK_DEV, TOK_DEV, NB * BS)
    zeros_sq = jnp.zeros((NB, BS, BS), jnp.float32)
    zeros_us = jnp.zeros((NB, BS, HB), jnp.float32)
    zeros_df = jnp.zeros((NB, HB, BS), jnp.float32)

    def step_block(carry, pieces):
        grads_out = window_pass(pieces[0], pieces[1], up_first, up_second, down_first, down_second)
        summed = tuple((carry[index] + grads_out[index + 1] for index in range(4)))
        return (summed, grads_out[0])
    totals, input_blocks = lax.scan(step_block, (zeros_sq, zeros_us, zeros_df, zeros_sq), (blocks_in, blocks_up))
    factor = 1.0 / math.sqrt(TOKENS)
    input_grad = input_blocks.reshape(TOKENS, NB * BS)
    return (input_grad, totals[0] * factor, totals[1] * factor, totals[2] * factor, totals[3] * factor)
```

```python
import functools
import math

import jax
import jax.numpy as jnp
from jax import lax
from jax.experimental import pallas as pl
from jax.experimental.pallas import tpu as pltpu
from jax.sharding import PartitionSpec as P

SIDE = 2
VMEM_BYTES = 50 * 1024 * 1024


class Place:
    def __init__(self, size):
        self.depth = size // SIDE
        me = lax.axis_index("dp")
        self.z = lax.div(me, SIDE)
        self.x = lax.rem(me, SIDE)
        self.me = me
        self.partner = self.z * SIDE + (1 - self.x)

    def chunk(self, z, x):
        return z * SIDE + x

    def has_below(self):
        return self.z > 0

    def has_above(self):
        return self.z < self.depth - 1


def greet(place):
    barrier = pltpu.get_barrier_semaphore()

    def tell(target):
        pl.semaphore_signal(
            barrier, inc=1, device_id={"dp": target}, device_id_type=pl.DeviceIdType.MESH
        )

    tell(place.partner)
    pl.when(place.has_below())(lambda: tell(place.me - SIDE))
    pl.when(place.has_above())(lambda: tell(place.me + SIDE))
    inner = jnp.logical_and(place.has_below(), place.has_above())
    pl.when(inner)(lambda: pl.semaphore_wait(barrier, 3))
    pl.when(jnp.logical_not(inner))(lambda: pl.semaphore_wait(barrier, 2))


def rows_of(ref, index, rows):
    return ref.at[:, pl.ds(pl.multiple_of(index * rows, rows), rows), :]


def send(src, dst, send_sem, recv_sem, target):
    return pltpu.make_async_remote_copy(
        src_ref=src,
        dst_ref=dst,
        send_sem=send_sem,
        recv_sem=recv_sem,
        device_id={"dp": target},
        device_id_type=pl.DeviceIdType.MESH,
    )


class Gather:
    def __init__(self, place, own, out, rows, local_sem, sends, recv, wide):
        self.p, self.own, self.out, self.rows, self.wide = place, own, out, rows, wide
        self.local_sem, self.sends, self.recv = local_sem, sends, recv

    def _copy(self, index, way, target):
        mine = rows_of(self.out, index, self.rows)
        return send(mine, mine, self.sends.at[way, index], self.recv.at[index], target)

    def _own(self, way, target):
        me = self.p.me
        return send(
            self.own,
            rows_of(self.out, me, self.rows),
            self.sends.at[way, me],
            self.recv.at[me],
            target,
        )

    def _local(self):
        return pltpu.make_async_copy(
            self.own, rows_of(self.out, self.p.me, self.rows), self.local_sem
        )

    def across(self, index):
        return self._copy(index, 0, self.p.partner)

    def up(self, index):
        return self._copy(index, 1, self.p.me + SIDE)

    def down(self, index):
        return self._copy(index, 2, self.p.me - SIDE)

    def begin(self):
        p = self.p
        pl.when(p.has_above())(lambda: self._own(1, p.me + SIDE).start())
        pl.when(p.has_below())(lambda: self._own(2, p.me - SIDE).start())
        self._own(0, p.partner).start()
        self._local().start()

    def landed(self, index):
        self._copy(index, 0, self.p.partner).wait_recv()

    def begin_wide(self):
        p = self.p
        if self.wide:
            self.landed(p.partner)
            pl.when(p.has_above())(lambda: self.up(p.partner).start())
            pl.when(p.has_below())(lambda: self.down(p.partner).start())

    def step(self, distance):
        p = self.p
        columns = (p.x, 1 - p.x) if self.wide else (p.x,)
        for x in columns:

            def from_below():
                index = p.chunk(p.z - distance, x)
                self.landed(index)
                pl.when(p.has_above())(lambda: self.up(index).start())
                if not self.wide:
                    self.across(index).start()

            def from_above():
                index = p.chunk(p.z + distance, x)
                self.landed(index)
                pl.when(p.has_below())(lambda: self.down(index).start())
                if not self.wide:
                    self.across(index).start()

            pl.when(p.z >= distance)(from_below)
            pl.when(p.z + distance < p.depth)(from_above)

    def finish(self):
        p = self.p
        if not self.wide:
            for z in range(p.depth):
                self.landed(p.chunk(z, 1 - p.x))
        self._local().wait()
        self._own(0, p.partner).wait_send()
        columns = (p.x, 1 - p.x) if self.wide else (p.x,)
        for x in columns:
            here = p.chunk(p.z, x)
            pl.when(p.has_above())(lambda: self.up(here).wait_send())
            pl.when(p.has_below())(lambda: self.down(here).wait_send())
            for distance in range(1, p.depth):

                def below():
                    index = p.chunk(p.z - distance, x)
                    pl.when(p.has_above())(lambda: self.up(index).wait_send())
                    if not self.wide:
                        self.across(index).wait_send()

                def above():
                    index = p.chunk(p.z + distance, x)
                    pl.when(p.has_below())(lambda: self.down(index).wait_send())
                    if not self.wide:
                        self.across(index).wait_send()

                pl.when(p.z >= distance)(below)
                pl.when(p.z + distance < p.depth)(above)


def run_gathers(gathers, depth):
    for gather in gathers:
        gather.begin()
    for gather in gathers:
        gather.begin_wide()
    for distance in range(1, depth):
        for gather in gathers:
            gather.step(distance)
    for gather in gathers:
        gather.finish()


def gather_kernel(size, count, *refs):
    owns, outs = refs[:count], refs[count : 2 * count]
    local, sends, recv = refs[2 * count :]
    place = Place(size)
    greet(place)
    gathers = [
        Gather(
            place, owns[a], outs[a], owns[a].shape[1],
            local.at[a], sends.at[a], recv.at[a], a == 0,
        )
        for a in range(count)
    ]
    run_gathers(gathers, place.depth)


def gather_rows(arrays, size):
    count = len(arrays)
    anywhere = pl.BlockSpec(memory_space=pl.ANY)
    return pl.pallas_call(
        functools.partial(gather_kernel, size, count),
        out_shape=tuple(
            jax.ShapeDtypeStruct((a.shape[0], a.shape[1] * size, a.shape[2]), a.dtype)
            for a in arrays
        ),
        in_specs=[anywhere] * count,
        out_specs=tuple([anywhere] * count),
        scratch_shapes=[
            pltpu.SemaphoreType.DMA((count,)),
            pltpu.SemaphoreType.DMA((count, 3, size)),
            pltpu.SemaphoreType.DMA((count, size)),
        ],
        compiler_params=pltpu.CompilerParams(collective_id=0, has_side_effects=True),
        name="gather_rows",
    )(*arrays)


class Reduce:
    def __init__(self, place, grad, rows, scale, final, cross, low, high, stage, sems):
        self.p, self.grad, self.rows, self.scale, self.final = place, grad, rows, scale, final
        self.cross, self.low, self.high, self.stage, self.sems = cross, low, high, stage, sems

    def _cross(self, z):
        p = self.p
        return send(
            rows_of(self.grad, p.chunk(z, 1 - p.x), self.rows),
            self.cross.at[z],
            self.sems.at[0, z],
            self.sems.at[1, z],
            p.partner,
        )

    def _up(self, z):
        return send(
            self.stage.at[z], self.low.at[z], self.sems.at[2, z], self.sems.at[3, z],
            self.p.me + SIDE,
        )

    def _down(self, z):
        return send(
            self.stage.at[z], self.high.at[z], self.sems.at[4, z], self.sems.at[5, z],
            self.p.me - SIDE,
        )

    def send_across(self, distance):
        p = self.p
        if distance == 0:
            self._cross(p.z).start()
            return
        pl.when(p.z + distance < p.depth)(lambda: self._cross(p.z + distance).start())
        pl.when(p.z >= distance)(lambda: self._cross(p.z - distance).start())

    def _sum(self, z, others, store):
        first = pl.multiple_of(self.p.chunk(z, self.p.x) * self.rows, self.rows)

        @pl.loop(0, self.grad.shape[0], unroll=2)
        def _(block):
            total = self.grad[block, pl.ds(first, self.rows), :].astype(jnp.float32)
            for other in (self.cross,) + others:
                total = total + other[z, block].astype(jnp.float32)
            store(block, total)

    def step(self, distance):
        p = self.p

        def upward():
            z = p.z + distance
            self._cross(z).wait_recv()

            def store(block, total):
                self.stage[z, block] = total.astype(self.stage.dtype)

            def joined():
                self._up(z).wait_recv()
                self._sum(z, (self.low,), store)

            pl.when(p.has_below())(joined)
            pl.when(jnp.logical_not(p.has_below()))(lambda: self._sum(z, (), store))
            self._up(z).start()

        def downward():
            z = p.z - distance
            self._cross(z).wait_recv()

            def store(block, total):
                self.stage[z, block] = total.astype(self.stage.dtype)

            def joined():
                self._down(z).wait_recv()
                self._sum(z, (self.high,), store)

            pl.when(p.has_above())(joined)
            pl.when(jnp.logical_not(p.has_above()))(lambda: self._sum(z, (), store))
            self._down(z).start()

        pl.when(p.z + distance < p.depth)(upward)
        pl.when(p.z >= distance)(downward)

    def last(self):
        p = self.p

        def store(block, total):
            self.final[block] = (total * self.scale).astype(self.final.dtype)

        self._cross(p.z).wait_recv()
        pl.when(p.has_below())(lambda: self._up(p.z).wait_recv())
        pl.when(p.has_above())(lambda: self._down(p.z).wait_recv())
        low, high = p.has_below(), p.has_above()
        pl.when(jnp.logical_and(low, high))(
            lambda: self._sum(p.z, (self.low, self.high), store)
        )
        pl.when(jnp.logical_not(high))(lambda: self._sum(p.z, (self.low,), store))
        pl.when(jnp.logical_not(low))(lambda: self._sum(p.z, (self.high,), store))

    def finish(self):
        p = self.p
        for z in range(p.depth):
            self._cross(z).wait_send()
        for distance in range(1, p.depth):
            pl.when(p.z + distance < p.depth)(lambda: self._up(p.z + distance).wait_send())
            pl.when(p.z >= distance)(lambda: self._down(p.z - distance).wait_send())


def reduce_kernel(size, scale, shared, *refs):
    count = 4
    grads, outs = refs[:count], refs[count : 2 * count]
    rest = refs[2 * count :]
    crosses, lows, highs, stages = (rest[k * count : (k + 1) * count] for k in range(4))
    finals = rest[4 * count : 4 * count + shared]
    sems, local, sends, recv = rest[4 * count + shared :]
    place = Place(size)
    greet(place)
    reduces = [
        Reduce(
            place, grads[a], grads[a].shape[1] // size, scale,
            finals[a] if a < shared else outs[a],
            crosses[a], lows[a], highs[a], stages[a], sems.at[a],
        )
        for a in range(count)
    ]
    gathers = [
        Gather(
            place, finals[a], outs[a], finals[a].shape[1],
            local.at[a], sends.at[a], recv.at[a], False,
        )
        for a in range(shared)
    ]
    for distance in range(place.depth - 1, -1, -1):
        for reduce in reduces:
            reduce.send_across(distance)
    for distance in range(place.depth - 1, 0, -1):
        for reduce in reduces:
            reduce.step(distance)
    for a in range(shared):
        reduces[a].last()
        gathers[a].begin()
    for a in range(shared, count):
        reduces[a].last()
    for distance in range(1, place.depth):
        for gather in gathers:
            gather.step(distance)
    for gather in gathers:
        gather.finish()
    for reduce in reduces:
        reduce.finish()


def reduce_rows(grads, shared, size, scale):
    depth = size // SIDE
    parts = [(g.shape[0], g.shape[1] // size, g.shape[2]) for g in grads]
    slots = [pltpu.VMEM((depth,) + part, jnp.bfloat16) for part in parts]
    vmem = pl.BlockSpec(memory_space=pltpu.VMEM)
    anywhere = pl.BlockSpec(memory_space=pl.ANY)
    count = len(grads)
    return pl.pallas_call(
        functools.partial(reduce_kernel, size, scale, shared),
        out_shape=tuple(
            jax.ShapeDtypeStruct(g.shape, jnp.bfloat16)
            if a < shared
            else jax.ShapeDtypeStruct(parts[a], jnp.float32)
            for a, g in enumerate(grads)
        ),
        in_specs=[vmem] * count,
        out_specs=tuple(anywhere if a < shared else vmem for a in range(count)),
        scratch_shapes=slots * 4
        + [pltpu.VMEM(parts[a], jnp.bfloat16) for a in range(shared)]
        + [
            pltpu.SemaphoreType.DMA((count, 6, depth)),
            pltpu.SemaphoreType.DMA((shared,)),
            pltpu.SemaphoreType.DMA((shared, 3, size)),
            pltpu.SemaphoreType.DMA((shared, size)),
        ],
        compiler_params=pltpu.CompilerParams(
            collective_id=1, has_side_effects=True, vmem_limit_bytes=VMEM_BYTES
        ),
        name="reduce_rows",
    )(*grads)


def activation(values):
    return jax.nn.gelu(values, approximate=True)


def permute_forward(lower, second):

    def apply_second(piece):
        if second is None:
            return (piece,)
        product = jnp.einsum("tbj,jbk->tjk", piece, second, preferred_element_type=jnp.float32)
        return (piece, product)

    return apply_second(lax.all_to_all(lower, "blk", split_axis=2, concat_axis=1, tiled=True))


def permute_backward(grad_out, second):
    spread = jnp.einsum(
        "tjk,jbk->tbj", grad_out, second, preferred_element_type=jnp.float32
    ).astype(jnp.bfloat16)
    return lax.all_to_all(spread, "blk", split_axis=1, concat_axis=2, tiled=True)


def per_device(tokens, up_first, up_second, down_first, down_second, cotangent):
    tok_rows = tokens.shape[0]
    local_blocks = up_first.shape[0]
    block_size = up_first.shape[2]
    factor = 1.0 / math.sqrt(tok_rows * lax.axis_size("dp"))
    size = lax.axis_size("dp")
    weights = (down_second, up_first, up_second, down_first)
    tiled = size % SIDE == 0 and size > SIDE and all(w.shape[1] % 16 == 0 for w in weights)
    if tiled:
        full_ds, full_uf, full_us, full_df = gather_rows(weights, size)
    else:
        full_ds, full_uf, full_us, full_df = (
            lax.all_gather(w, "dp", axis=1, tiled=True) for w in weights
        )
    inputs_b = tokens.reshape(tok_rows, local_blocks, block_size)
    first_up = jnp.einsum(
        "tbi,bij->tbj", inputs_b, full_uf, preferred_element_type=jnp.float32
    ).astype(jnp.bfloat16)
    moved_up, pre_act = permute_forward(first_up, full_us)
    hidden = activation(pre_act).astype(jnp.bfloat16)
    first_down = jnp.einsum(
        "tbi,bij->tbj", hidden, full_df, preferred_element_type=jnp.float32
    ).astype(jnp.bfloat16)
    moved_down = permute_forward(first_down, None)[0]
    upstream = cotangent.reshape(tok_rows, local_blocks, block_size)
    grad_ds = jnp.einsum("tbj,tjk->jbk", moved_down, upstream, preferred_element_type=jnp.float32)
    back_down = permute_backward(upstream, full_ds)
    grad_df = jnp.einsum("tbi,tbj->bij", hidden, back_down, preferred_element_type=jnp.float32)
    hidden_grad = jnp.einsum("tbj,bij->tbi", back_down, full_df, preferred_element_type=jnp.float32)
    _, pull_back = jax.vjp(activation, pre_act)
    pre_grad = pull_back(hidden_grad)[0].astype(jnp.bfloat16)
    grad_us = jnp.einsum("tbj,tjk->jbk", moved_up, pre_grad, preferred_element_type=jnp.float32)
    back_up = permute_backward(pre_grad, full_us)
    grad_uf = jnp.einsum("tbi,tbj->bij", inputs_b, back_up, preferred_element_type=jnp.float32)
    input_grad = jnp.einsum(
        "tbj,bij->tbi", back_up, full_uf, preferred_element_type=jnp.float32
    ).astype(jnp.bfloat16)
    input_grad = input_grad.reshape(tok_rows, local_blocks * block_size)
    if tiled:
        grads = (grad_ds, grad_uf, grad_us, grad_df)
        grad_ds, grad_uf, grad_us, grad_df = reduce_rows(
            tuple(g.astype(jnp.bfloat16) for g in grads), 2, size, factor
        )
        grad_ds = grad_ds.astype(jnp.float32)
        grad_uf = grad_uf.astype(jnp.float32)
        return (input_grad, grad_uf, grad_us, grad_df, grad_ds)
    wide_sum = (
        lax.psum_scatter(grad_us, "dp", scatter_dimension=1, tiled=True),
        lax.psum_scatter(grad_df, "dp", scatter_dimension=1, tiled=True),
    )
    square_sum = lax.psum((grad_uf, grad_ds), "dp")
    grad_us = wide_sum[0] * factor
    grad_df = wide_sum[1] * factor
    grad_uf = square_sum[0] * factor
    grad_ds = square_sum[1] * factor
    return (input_grad, grad_uf, grad_us, grad_df, grad_ds)


def solution(mesh):
    placed = (
        P("dp", "blk"),
        P("blk", "dp", None),
        P("blk", "dp", None),
        P("blk", "dp", None),
        P("blk", "dp", None),
        P("dp", "blk"),
    )
    return jax.shard_map(
        per_device,
        mesh=mesh,
        in_specs=placed,
        out_specs=(
            P("dp", "blk"),
            P("blk", None, None),
            P("blk", "dp", None),
            P("blk", "dp", None),
            P("blk", None, None),
        ),
        check_vma=False,
    )
```

```python
import functools
import math

import jax
import jax.numpy as jnp
from jax import lax
from jax.experimental import pallas as pl
from jax.experimental.pallas import tpu as pltpu
from jax.sharding import PartitionSpec as P

SIDE = 2
VMEM_BYTES = 50 * 1024 * 1024


class Place:
    def __init__(self, size):
        self.depth = size // SIDE
        me = lax.axis_index("dp")
        self.z = lax.div(me, SIDE)
        self.x = lax.rem(me, SIDE)
        self.me = me
        self.partner = self.z * SIDE + (1 - self.x)

    def chunk(self, z, x):
        return z * SIDE + x

    def has_below(self):
        return self.z > 0

    def has_above(self):
        return self.z < self.depth - 1


def greet(place):
    barrier = pltpu.get_barrier_semaphore()

    def tell(target):
        pl.semaphore_signal(
            barrier, inc=1, device_id={"dp": target}, device_id_type=pl.DeviceIdType.MESH
        )

    tell(place.partner)
    pl.when(place.has_below())(lambda: tell(place.me - SIDE))
    pl.when(place.has_above())(lambda: tell(place.me + SIDE))
    spread = lax.axis_size("blk")
    for hop in range(1, spread):
        pl.semaphore_signal(
            barrier,
            inc=1,
            device_id={"blk": lax.rem(lax.axis_index("blk") + hop, spread)},
            device_id_type=pl.DeviceIdType.MESH,
        )
    inner = jnp.logical_and(place.has_below(), place.has_above())
    pl.when(inner)(lambda: pl.semaphore_wait(barrier, spread + 2))
    pl.when(jnp.logical_not(inner))(lambda: pl.semaphore_wait(barrier, spread + 1))


def rows_of(ref, index, rows):
    return ref.at[:, pl.ds(pl.multiple_of(index * rows, rows), rows), :]


def send(src, dst, send_sem, recv_sem, target):
    return pltpu.make_async_remote_copy(
        src_ref=src,
        dst_ref=dst,
        send_sem=send_sem,
        recv_sem=recv_sem,
        device_id={"dp": target},
        device_id_type=pl.DeviceIdType.MESH,
    )


class Gather:
    def __init__(self, place, own, out, rows, local_sem, sends, recv, wide):
        self.p, self.own, self.out, self.rows, self.wide = place, own, out, rows, wide
        self.local_sem, self.sends, self.recv = local_sem, sends, recv

    def _copy(self, index, way, target):
        mine = rows_of(self.out, index, self.rows)
        return send(mine, mine, self.sends.at[way, index], self.recv.at[index], target)

    def _own(self, way, target):
        me = self.p.me
        return send(
            self.own,
            rows_of(self.out, me, self.rows),
            self.sends.at[way, me],
            self.recv.at[me],
            target,
        )

    def _local(self):
        return pltpu.make_async_copy(
            self.own, rows_of(self.out, self.p.me, self.rows), self.local_sem
        )

    def across(self, index):
        return self._copy(index, 0, self.p.partner)

    def up(self, index):
        return self._copy(index, 1, self.p.me + SIDE)

    def down(self, index):
        return self._copy(index, 2, self.p.me - SIDE)

    def begin(self):
        p = self.p
        pl.when(p.has_above())(lambda: self._own(1, p.me + SIDE).start())
        pl.when(p.has_below())(lambda: self._own(2, p.me - SIDE).start())
        self._own(0, p.partner).start()
        self._local().start()

    def landed(self, index):
        self._copy(index, 0, self.p.partner).wait_recv()

    def begin_wide(self):
        p = self.p
        if self.wide:
            self.landed(p.partner)
            pl.when(p.has_above())(lambda: self.up(p.partner).start())
            pl.when(p.has_below())(lambda: self.down(p.partner).start())

    def step(self, distance):
        p = self.p
        columns = (p.x, 1 - p.x) if self.wide else (p.x,)
        for x in columns:

            def from_below():
                index = p.chunk(p.z - distance, x)
                self.landed(index)
                pl.when(p.has_above())(lambda: self.up(index).start())
                if not self.wide:
                    self.across(index).start()

            def from_above():
                index = p.chunk(p.z + distance, x)
                self.landed(index)
                pl.when(p.has_below())(lambda: self.down(index).start())
                if not self.wide:
                    self.across(index).start()

            pl.when(p.z >= distance)(from_below)
            pl.when(p.z + distance < p.depth)(from_above)

    def finish(self):
        p = self.p
        if not self.wide:
            for z in range(p.depth):
                self.landed(p.chunk(z, 1 - p.x))
        self._local().wait()
        self._own(0, p.partner).wait_send()
        columns = (p.x, 1 - p.x) if self.wide else (p.x,)
        for x in columns:
            here = p.chunk(p.z, x)
            pl.when(p.has_above())(lambda: self.up(here).wait_send())
            pl.when(p.has_below())(lambda: self.down(here).wait_send())
            for distance in range(1, p.depth):

                def below():
                    index = p.chunk(p.z - distance, x)
                    pl.when(p.has_above())(lambda: self.up(index).wait_send())
                    if not self.wide:
                        self.across(index).wait_send()

                def above():
                    index = p.chunk(p.z + distance, x)
                    pl.when(p.has_below())(lambda: self.down(index).wait_send())
                    if not self.wide:
                        self.across(index).wait_send()

                pl.when(p.z >= distance)(below)
                pl.when(p.z + distance < p.depth)(above)


class Exchange:
    def __init__(self, made, out, local_sem, sends, recv):
        self.made, self.out, self.local_sem, self.sends, self.recv = made, out, local_sem, sends, recv
        self.count = lax.axis_size("blk")
        self.blocks = made.shape[0]
        self.part = made.shape[1] // self.count
        self.me = lax.axis_index("blk")

    def _copy(self, hop):
        target = lax.rem(self.me + hop, self.count)
        return pltpu.make_async_remote_copy(
            src_ref=rows_of(self.made, target, self.part),
            dst_ref=self.out.at[pl.ds(self.me * self.blocks, self.blocks)],
            send_sem=self.sends.at[hop],
            recv_sem=self.recv.at[hop],
            device_id={"blk": target},
            device_id_type=pl.DeviceIdType.MESH,
        )

    def _local(self):
        return pltpu.make_async_copy(
            rows_of(self.made, self.me, self.part),
            self.out.at[pl.ds(self.me * self.blocks, self.blocks)],
            self.local_sem,
        )

    def begin(self):
        for hop in range(1, self.count):
            self._copy(hop).start()
        self._local().start()

    def finish(self):
        for hop in range(1, self.count):
            self._copy(hop).wait()
        self._local().wait()


def gather_kernel(size, *refs):
    count = 4
    owns, tokens, upstream = refs[:count], refs[count], refs[count + 1]
    outs, moved_down, moved_up = refs[6 : 6 + count], refs[6 + count], refs[7 + count]
    local, sends, recv, back, first, local_blk, sends_blk, recv_blk = refs[8 + count :]
    place = Place(size)
    greet(place)
    gathers = [
        Gather(
            place, owns[a], outs[a], owns[a].shape[1],
            local.at[a], sends.at[a], recv.at[a], a == 0,
        )
        for a in range(count)
    ]
    down = Exchange(back, moved_down, local_blk.at[0], sends_blk.at[0], recv_blk.at[0])
    up = Exchange(first, moved_up, local_blk.at[1], sends_blk.at[1], recv_blk.at[1])
    blocks, width = first.shape[0], first.shape[1]
    for gather in gathers:
        gather.begin()
    gathers[0].begin_wide()
    for distance in range(1, place.depth):
        for gather in gathers[:2]:
            gather.step(distance)
        if distance < place.depth - 1:
            for gather in gathers[2:]:
                gather.step(distance)
    gathers[0].finish()

    @pl.loop(0, blocks, unroll=2)
    def _(block):
        columns = pl.ds(pl.multiple_of(block * width, width), width)
        back[block] = lax.dot_general(
            outs[0][block], upstream[:, columns], (((1,), (1,)), ((), ())),
            preferred_element_type=jnp.float32,
        ).astype(jnp.bfloat16)

    down.begin()
    for gather in gathers[2:]:
        gather.step(place.depth - 1)
    gathers[1].finish()

    @pl.loop(0, blocks, unroll=2)
    def _(block):
        columns = pl.ds(pl.multiple_of(block * width, width), width)
        product = jnp.dot(
            tokens[:, columns], outs[1][block], preferred_element_type=jnp.float32
        )
        first[block] = product.T.astype(jnp.bfloat16)

    up.begin()
    for gather in gathers[2:]:
        gather.finish()
    down.finish()
    up.finish()


def gather_rows(arrays, tokens, upstream, size):
    count = len(arrays)
    vmem = pl.BlockSpec(memory_space=pltpu.VMEM)
    anywhere = pl.BlockSpec(memory_space=pl.ANY)
    spread = lax.axis_size("blk")
    blocks, width, rows = arrays[0].shape[0], arrays[0].shape[2], tokens.shape[0]
    moved = jax.ShapeDtypeStruct((blocks * spread, width // spread, rows), jnp.bfloat16)
    return pl.pallas_call(
        functools.partial(gather_kernel, size),
        out_shape=tuple(
            jax.ShapeDtypeStruct((a.shape[0], a.shape[1] * size, a.shape[2]), a.dtype)
            for a in arrays
        )
        + (moved, moved),
        in_specs=[anywhere] * count + [vmem, vmem],
        out_specs=(vmem, vmem) + (anywhere,) * (count - 2) + (anywhere, anywhere),
        scratch_shapes=[
            pltpu.SemaphoreType.DMA((count,)),
            pltpu.SemaphoreType.DMA((count, 3, size)),
            pltpu.SemaphoreType.DMA((count, size)),
            pltpu.VMEM((blocks, width, rows), jnp.bfloat16),
            pltpu.VMEM((blocks, width, rows), jnp.bfloat16),
            pltpu.SemaphoreType.DMA((2,)),
            pltpu.SemaphoreType.DMA((2, spread)),
            pltpu.SemaphoreType.DMA((2, spread)),
        ],
        compiler_params=pltpu.CompilerParams(
            collective_id=0, has_side_effects=True, vmem_limit_bytes=VMEM_BYTES
        ),
        name="gather_rows",
    )(*arrays, tokens, upstream)


class Reduce:
    def __init__(self, place, grad, rows, scale, final, cross, low, high, stage, sems):
        self.p, self.grad, self.rows, self.scale, self.final = place, grad, rows, scale, final
        self.cross, self.low, self.high, self.stage, self.sems = cross, low, high, stage, sems

    def _cross(self, z):
        p = self.p
        return send(
            rows_of(self.grad, p.chunk(z, 1 - p.x), self.rows),
            self.cross.at[z],
            self.sems.at[0, z],
            self.sems.at[1, z],
            p.partner,
        )

    def _up(self, z):
        return send(
            self.stage.at[z], self.low.at[z], self.sems.at[2, z], self.sems.at[3, z],
            self.p.me + SIDE,
        )

    def _down(self, z):
        return send(
            self.stage.at[z], self.high.at[z], self.sems.at[4, z], self.sems.at[5, z],
            self.p.me - SIDE,
        )

    def send_across(self, distance):
        p = self.p
        if distance == 0:
            self._cross(p.z).start()
            return
        pl.when(p.z + distance < p.depth)(lambda: self._cross(p.z + distance).start())
        pl.when(p.z >= distance)(lambda: self._cross(p.z - distance).start())

    def _sum(self, z, others, store):
        first = pl.multiple_of(self.p.chunk(z, self.p.x) * self.rows, self.rows)

        @pl.loop(0, self.grad.shape[0], unroll=2)
        def _(block):
            total = self.grad[block, pl.ds(first, self.rows), :].astype(jnp.float32)
            for other in (self.cross,) + others:
                total = total + other[z, block].astype(jnp.float32)
            store(block, total)

    def step(self, distance):
        p = self.p

        def upward():
            z = p.z + distance
            self._cross(z).wait_recv()

            def store(block, total):
                self.stage[z, block] = total.astype(self.stage.dtype)

            def joined():
                self._up(z).wait_recv()
                self._sum(z, (self.low,), store)

            pl.when(p.has_below())(joined)
            pl.when(jnp.logical_not(p.has_below()))(lambda: self._sum(z, (), store))
            self._up(z).start()

        def downward():
            z = p.z - distance
            self._cross(z).wait_recv()

            def store(block, total):
                self.stage[z, block] = total.astype(self.stage.dtype)

            def joined():
                self._down(z).wait_recv()
                self._sum(z, (self.high,), store)

            pl.when(p.has_above())(joined)
            pl.when(jnp.logical_not(p.has_above()))(lambda: self._sum(z, (), store))
            self._down(z).start()

        pl.when(p.z + distance < p.depth)(upward)
        pl.when(p.z >= distance)(downward)

    def last(self):
        p = self.p

        def store(block, total):
            self.final[block] = (total * self.scale).astype(self.final.dtype)

        self._cross(p.z).wait_recv()
        pl.when(p.has_below())(lambda: self._up(p.z).wait_recv())
        pl.when(p.has_above())(lambda: self._down(p.z).wait_recv())
        low, high = p.has_below(), p.has_above()
        pl.when(jnp.logical_and(low, high))(
            lambda: self._sum(p.z, (self.low, self.high), store)
        )
        pl.when(jnp.logical_not(high))(lambda: self._sum(p.z, (self.low,), store))
        pl.when(jnp.logical_not(low))(lambda: self._sum(p.z, (self.high,), store))

    def finish(self):
        p = self.p
        for z in range(p.depth):
            self._cross(z).wait_send()
        for distance in range(1, p.depth):
            pl.when(p.z + distance < p.depth)(lambda: self._up(p.z + distance).wait_send())
            pl.when(p.z >= distance)(lambda: self._down(p.z - distance).wait_send())


def reduce_kernel(size, scale, shared, *refs):
    count = 4
    grads, outs = refs[:count], refs[count : 2 * count]
    rest = refs[2 * count :]
    crosses, lows, highs, stages = (rest[k * count : (k + 1) * count] for k in range(4))
    finals = rest[4 * count : 4 * count + shared]
    sems, local, sends, recv = rest[4 * count + shared :]
    place = Place(size)
    greet(place)
    reduces = [
        Reduce(
            place, grads[a], grads[a].shape[1] // size, scale,
            finals[a] if a < shared else outs[a],
            crosses[a], lows[a], highs[a], stages[a], sems.at[a],
        )
        for a in range(count)
    ]
    gathers = [
        Gather(
            place, finals[a], outs[a], finals[a].shape[1],
            local.at[a], sends.at[a], recv.at[a], False,
        )
        for a in range(shared)
    ]
    for distance in range(place.depth - 1, -1, -1):
        for reduce in reduces:
            reduce.send_across(distance)
    for distance in range(place.depth - 1, 0, -1):
        for reduce in reduces:
            reduce.step(distance)
    for a in range(shared):
        reduces[a].last()
        gathers[a].begin()
    for a in range(shared, count):
        reduces[a].last()
    for distance in range(1, place.depth):
        for gather in gathers:
            gather.step(distance)
    for gather in gathers:
        gather.finish()
    for reduce in reduces:
        reduce.finish()


def reduce_rows(grads, shared, size, scale):
    depth = size // SIDE
    parts = [(g.shape[0], g.shape[1] // size, g.shape[2]) for g in grads]
    slots = [pltpu.VMEM((depth,) + part, jnp.bfloat16) for part in parts]
    vmem = pl.BlockSpec(memory_space=pltpu.VMEM)
    anywhere = pl.BlockSpec(memory_space=pl.ANY)
    count = len(grads)
    return pl.pallas_call(
        functools.partial(reduce_kernel, size, scale, shared),
        out_shape=tuple(
            jax.ShapeDtypeStruct(g.shape, jnp.bfloat16)
            if a < shared
            else jax.ShapeDtypeStruct(parts[a], jnp.float32)
            for a, g in enumerate(grads)
        ),
        in_specs=[vmem] * count,
        out_specs=tuple(anywhere if a < shared else vmem for a in range(count)),
        scratch_shapes=slots * 4
        + [pltpu.VMEM(parts[a], jnp.bfloat16) for a in range(shared)]
        + [
            pltpu.SemaphoreType.DMA((count, 6, depth)),
            pltpu.SemaphoreType.DMA((shared,)),
            pltpu.SemaphoreType.DMA((shared, 3, size)),
            pltpu.SemaphoreType.DMA((shared, size)),
        ],
        compiler_params=pltpu.CompilerParams(
            collective_id=1, has_side_effects=True, vmem_limit_bytes=VMEM_BYTES
        ),
        name="reduce_rows",
    )(*grads)


def activation(values):
    return jax.nn.gelu(values, approximate=True)


def permute_forward(lower, second):

    def apply_second(piece):
        if second is None:
            return (piece,)
        product = jnp.einsum("tbj,jbk->tjk", piece, second, preferred_element_type=jnp.float32)
        return (piece, product)

    return apply_second(lax.all_to_all(lower, "blk", split_axis=2, concat_axis=1, tiled=True))


def permute_backward(grad_out, second):
    spread = jnp.einsum(
        "tjk,jbk->tbj", grad_out, second, preferred_element_type=jnp.float32
    ).astype(jnp.bfloat16)
    return lax.all_to_all(spread, "blk", split_axis=1, concat_axis=2, tiled=True)


def by_collectives(tokens, up_first, up_second, down_first, down_second, cotangent):
    tok_rows = tokens.shape[0]
    local_blocks = up_first.shape[0]
    block_size = up_first.shape[2]
    factor = 1.0 / math.sqrt(tok_rows * lax.axis_size("dp"))
    gathered = (
        lax.all_gather(up_first, "dp", axis=1, tiled=True),
        lax.all_gather(up_second, "dp", axis=1, tiled=True),
        lax.all_gather(down_first, "dp", axis=1, tiled=True),
        lax.all_gather(down_second, "dp", axis=1, tiled=True),
    )
    full_uf, full_us, full_df, full_ds = gathered
    inputs_b = tokens.reshape(tok_rows, local_blocks, block_size)
    first_up = jnp.einsum(
        "tbi,bij->tbj", inputs_b, full_uf, preferred_element_type=jnp.float32
    ).astype(jnp.bfloat16)
    moved_up, pre_act = permute_forward(first_up, full_us)
    hidden = activation(pre_act).astype(jnp.bfloat16)
    first_down = jnp.einsum(
        "tbi,bij->tbj", hidden, full_df, preferred_element_type=jnp.float32
    ).astype(jnp.bfloat16)
    moved_down = permute_forward(first_down, None)[0]
    upstream = cotangent.reshape(tok_rows, local_blocks, block_size)
    grad_ds = jnp.einsum("tbj,tjk->jbk", moved_down, upstream, preferred_element_type=jnp.float32)
    back_down = permute_backward(upstream, full_ds)
    grad_df = jnp.einsum("tbi,tbj->bij", hidden, back_down, preferred_element_type=jnp.float32)
    hidden_grad = jnp.einsum("tbj,bij->tbi", back_down, full_df, preferred_element_type=jnp.float32)
    _, pull_back = jax.vjp(activation, pre_act)
    pre_grad = pull_back(hidden_grad)[0].astype(jnp.bfloat16)
    grad_us = jnp.einsum("tbj,tjk->jbk", moved_up, pre_grad, preferred_element_type=jnp.float32)
    back_up = permute_backward(pre_grad, full_us)
    grad_uf = jnp.einsum("tbi,tbj->bij", inputs_b, back_up, preferred_element_type=jnp.float32)
    input_grad = jnp.einsum(
        "tbj,bij->tbi", back_up, full_uf, preferred_element_type=jnp.float32
    ).astype(jnp.bfloat16)
    input_grad = input_grad.reshape(tok_rows, local_blocks * block_size)
    wide_sum = (
        lax.psum_scatter(grad_us, "dp", scatter_dimension=1, tiled=True),
        lax.psum_scatter(grad_df, "dp", scatter_dimension=1, tiled=True),
    )
    square_sum = lax.psum((grad_uf, grad_ds), "dp")
    grad_us = wide_sum[0] * factor
    grad_df = wide_sum[1] * factor
    grad_uf = square_sum[0] * factor
    grad_ds = square_sum[1] * factor
    return (input_grad, grad_uf, grad_us, grad_df, grad_ds)


def per_device(tokens, up_first, up_second, down_first, down_second, cotangent):
    size, spread = lax.axis_size("dp"), lax.axis_size("blk")
    tok_rows = tokens.shape[0]
    local_blocks, _, block_size = up_first.shape
    weights = (down_second, up_first, up_second, down_first)
    tiled = (
        size % SIDE == 0
        and size > SIDE
        and spread > 1
        and all(w.shape[1] % 16 == 0 for w in weights)
        and block_size % (16 * spread) == 0
        and block_size == local_blocks * spread
    )
    if not tiled:
        return by_collectives(tokens, up_first, up_second, down_first, down_second, cotangent)
    factor = 1.0 / math.sqrt(tok_rows * size)
    full_ds, full_uf, full_us, full_df, back_down, moved_up = gather_rows(
        weights, tokens, cotangent, size
    )
    inputs_b = tokens.reshape(tok_rows, local_blocks, block_size)
    upstream = cotangent.reshape(tok_rows, local_blocks, block_size)
    pre_act = jnp.einsum("bjt,jbk->tjk", moved_up, full_us, preferred_element_type=jnp.float32)
    hidden = activation(pre_act).astype(jnp.bfloat16)
    hidden_grad = jnp.einsum("jbt,bij->tbi", back_down, full_df, preferred_element_type=jnp.float32)
    _, pull_back = jax.vjp(activation, pre_act)
    pre_grad = pull_back(hidden_grad)[0].astype(jnp.bfloat16)
    first_down = jnp.einsum(
        "tbi,bij->tbj", hidden, full_df, preferred_element_type=jnp.float32
    ).astype(jnp.bfloat16)
    moved_down = permute_forward(first_down, None)[0]
    back_up = permute_backward(pre_grad, full_us)
    grad_ds = jnp.einsum("tbj,tjk->jbk", moved_down, upstream, preferred_element_type=jnp.float32)
    grad_df = jnp.einsum("tbi,jbt->bij", hidden, back_down, preferred_element_type=jnp.float32)
    grad_us = jnp.einsum("bjt,tjk->jbk", moved_up, pre_grad, preferred_element_type=jnp.float32)
    grad_uf = jnp.einsum("tbi,tbj->bij", inputs_b, back_up, preferred_element_type=jnp.float32)
    input_grad = jnp.einsum(
        "tbj,bij->tbi", back_up, full_uf, preferred_element_type=jnp.float32
    ).astype(jnp.bfloat16)
    input_grad = input_grad.reshape(tok_rows, local_blocks * block_size)
    grads = (grad_ds, grad_uf, grad_us, grad_df)
    grad_ds, grad_uf, grad_us, grad_df = reduce_rows(
        tuple(g.astype(jnp.bfloat16) for g in grads), 2, size, factor
    )
    return (
        input_grad,
        grad_uf.astype(jnp.float32),
        grad_us,
        grad_df,
        grad_ds.astype(jnp.float32),
    )


def solution(mesh):
    placed = (
        P("dp", "blk"),
        P("blk", "dp", None),
        P("blk", "dp", None),
        P("blk", "dp", None),
        P("blk", "dp", None),
        P("dp", "blk"),
    )
    return jax.shard_map(
        per_device,
        mesh=mesh,
        in_specs=placed,
        out_specs=(
            P("dp", "blk"),
            P("blk", None, None),
            P("blk", "dp", None),
            P("blk", "dp", None),
            P("blk", None, None),
        ),
        check_vma=False,
    )
```

```python
import functools
import math

import jax
import jax.numpy as jnp
from jax import lax
from jax.experimental import pallas as pl
from jax.experimental.pallas import tpu as pltpu
from jax.sharding import PartitionSpec as P

SIDE = 2
VMEM_BYTES = 50 * 1024 * 1024


class Place:
    def __init__(self, size):
        self.depth = size // SIDE
        me = lax.axis_index("dp")
        self.z = lax.div(me, SIDE)
        self.x = lax.rem(me, SIDE)
        self.me = me
        self.partner = self.z * SIDE + (1 - self.x)

    def chunk(self, z, x):
        return z * SIDE + x

    def has_below(self):
        return self.z > 0

    def has_above(self):
        return self.z < self.depth - 1


def greet(place):
    barrier = pltpu.get_barrier_semaphore()

    def tell(target):
        pl.semaphore_signal(
            barrier, inc=1, device_id={"dp": target}, device_id_type=pl.DeviceIdType.MESH
        )

    tell(place.partner)
    pl.when(place.has_below())(lambda: tell(place.me - SIDE))
    pl.when(place.has_above())(lambda: tell(place.me + SIDE))
    spread = lax.axis_size("blk")
    for hop in range(1, spread):
        pl.semaphore_signal(
            barrier,
            inc=1,
            device_id={"blk": lax.rem(lax.axis_index("blk") + hop, spread)},
            device_id_type=pl.DeviceIdType.MESH,
        )
    inner = jnp.logical_and(place.has_below(), place.has_above())
    pl.when(inner)(lambda: pl.semaphore_wait(barrier, spread + 2))
    pl.when(jnp.logical_not(inner))(lambda: pl.semaphore_wait(barrier, spread + 1))


def rows_of(ref, index, rows):
    return ref.at[:, pl.ds(pl.multiple_of(index * rows, rows), rows), :]


def send(src, dst, send_sem, recv_sem, target):
    return pltpu.make_async_remote_copy(
        src_ref=src,
        dst_ref=dst,
        send_sem=send_sem,
        recv_sem=recv_sem,
        device_id={"dp": target},
        device_id_type=pl.DeviceIdType.MESH,
    )


class Gather:
    def __init__(self, place, own, out, rows, local_sem, sends, recv, wide):
        self.p, self.own, self.out, self.rows, self.wide = place, own, out, rows, wide
        self.local_sem, self.sends, self.recv = local_sem, sends, recv

    def _copy(self, index, way, target):
        mine = rows_of(self.out, index, self.rows)
        return send(mine, mine, self.sends.at[way, index], self.recv.at[index], target)

    def _own(self, way, target):
        me = self.p.me
        return send(
            self.own,
            rows_of(self.out, me, self.rows),
            self.sends.at[way, me],
            self.recv.at[me],
            target,
        )

    def _local(self):
        return pltpu.make_async_copy(
            self.own, rows_of(self.out, self.p.me, self.rows), self.local_sem
        )

    def across(self, index):
        return self._copy(index, 0, self.p.partner)

    def up(self, index):
        return self._copy(index, 1, self.p.me + SIDE)

    def down(self, index):
        return self._copy(index, 2, self.p.me - SIDE)

    def begin(self):
        p = self.p
        pl.when(p.has_above())(lambda: self._own(1, p.me + SIDE).start())
        pl.when(p.has_below())(lambda: self._own(2, p.me - SIDE).start())
        self._own(0, p.partner).start()
        self._local().start()

    def landed(self, index):
        self._copy(index, 0, self.p.partner).wait_recv()

    def begin_wide(self):
        p = self.p
        if self.wide:
            self.landed(p.partner)
            pl.when(p.has_above())(lambda: self.up(p.partner).start())
            pl.when(p.has_below())(lambda: self.down(p.partner).start())

    def step(self, distance):
        p = self.p
        columns = (p.x, 1 - p.x) if self.wide else (p.x,)
        for x in columns:

            def from_below():
                index = p.chunk(p.z - distance, x)
                self.landed(index)
                pl.when(p.has_above())(lambda: self.up(index).start())
                if not self.wide:
                    self.across(index).start()

            def from_above():
                index = p.chunk(p.z + distance, x)
                self.landed(index)
                pl.when(p.has_below())(lambda: self.down(index).start())
                if not self.wide:
                    self.across(index).start()

            pl.when(p.z >= distance)(from_below)
            pl.when(p.z + distance < p.depth)(from_above)

    def finish(self):
        p = self.p
        if not self.wide:
            for z in range(p.depth):
                self.landed(p.chunk(z, 1 - p.x))
        self._local().wait()
        self._own(0, p.partner).wait_send()
        columns = (p.x, 1 - p.x) if self.wide else (p.x,)
        for x in columns:
            here = p.chunk(p.z, x)
            pl.when(p.has_above())(lambda: self.up(here).wait_send())
            pl.when(p.has_below())(lambda: self.down(here).wait_send())
            for distance in range(1, p.depth):

                def below():
                    index = p.chunk(p.z - distance, x)
                    pl.when(p.has_above())(lambda: self.up(index).wait_send())
                    if not self.wide:
                        self.across(index).wait_send()

                def above():
                    index = p.chunk(p.z + distance, x)
                    pl.when(p.has_below())(lambda: self.down(index).wait_send())
                    if not self.wide:
                        self.across(index).wait_send()

                pl.when(p.z >= distance)(below)
                pl.when(p.z + distance < p.depth)(above)


class Exchange:
    def __init__(self, made, out, local_sem, sends, recv, leading=False):
        self.leading = leading
        self.made, self.out, self.local_sem, self.sends, self.recv = made, out, local_sem, sends, recv
        self.count = lax.axis_size("blk")
        self.blocks = made.shape[1 if leading else 0]
        self.part = made.shape[0 if leading else 1] // self.count
        self.me = lax.axis_index("blk")

    def _piece(self, target):
        if self.leading:
            return self.made.at[pl.ds(target * self.part, self.part)]
        return rows_of(self.made, target, self.part)

    def _place(self):
        if self.leading:
            return rows_of(self.out, self.me, self.blocks)
        return self.out.at[pl.ds(self.me * self.blocks, self.blocks)]

    def _copy(self, hop):
        target = lax.rem(self.me + hop, self.count)
        return pltpu.make_async_remote_copy(
            src_ref=self._piece(target),
            dst_ref=self._place(),
            send_sem=self.sends.at[hop],
            recv_sem=self.recv.at[hop],
            device_id={"blk": target},
            device_id_type=pl.DeviceIdType.MESH,
        )

    def _local(self):
        return pltpu.make_async_copy(self._piece(self.me), self._place(), self.local_sem)

    def begin(self):
        for hop in range(1, self.count):
            self._copy(hop).start()
        self._local().start()

    def finish(self):
        for hop in range(1, self.count):
            self._copy(hop).wait()
        self._local().wait()


def gather_kernel(size, *refs):
    count = 4
    owns, tokens, upstream = refs[:count], refs[count], refs[count + 1]
    outs, moved_down, moved_up = refs[6 : 6 + count], refs[6 + count], refs[7 + count]
    local, sends, recv, back, first, local_blk, sends_blk, recv_blk = refs[8 + count :]
    place = Place(size)
    greet(place)
    gathers = [
        Gather(
            place, owns[a], outs[a], owns[a].shape[1],
            local.at[a], sends.at[a], recv.at[a], a == 0,
        )
        for a in range(count)
    ]
    down = Exchange(back, moved_down, local_blk.at[0], sends_blk.at[0], recv_blk.at[0])
    up = Exchange(first, moved_up, local_blk.at[1], sends_blk.at[1], recv_blk.at[1])
    blocks, width = first.shape[0], first.shape[1]
    for gather in gathers:
        gather.begin()
    gathers[0].begin_wide()
    for distance in range(1, place.depth):
        for gather in gathers[:2]:
            gather.step(distance)
        if distance < place.depth - 1:
            for gather in gathers[2:]:
                gather.step(distance)
    gathers[0].finish()

    @pl.loop(0, blocks, unroll=2)
    def _(block):
        columns = pl.ds(pl.multiple_of(block * width, width), width)
        back[block] = lax.dot_general(
            outs[0][block], upstream[:, columns], (((1,), (1,)), ((), ())),
            preferred_element_type=jnp.float32,
        ).astype(jnp.bfloat16)

    down.begin()
    for gather in gathers[2:]:
        gather.step(place.depth - 1)
    gathers[1].finish()

    @pl.loop(0, blocks, unroll=2)
    def _(block):
        columns = pl.ds(pl.multiple_of(block * width, width), width)
        product = jnp.dot(
            tokens[:, columns], outs[1][block], preferred_element_type=jnp.float32
        )
        first[block] = product.T.astype(jnp.bfloat16)

    up.begin()
    for gather in gathers[2:]:
        gather.finish()
    down.finish()
    up.finish()


def gather_rows(arrays, tokens, upstream, size):
    count = len(arrays)
    vmem = pl.BlockSpec(memory_space=pltpu.VMEM)
    anywhere = pl.BlockSpec(memory_space=pl.ANY)
    spread = lax.axis_size("blk")
    blocks, width, rows = arrays[0].shape[0], arrays[0].shape[2], tokens.shape[0]
    moved = jax.ShapeDtypeStruct((blocks * spread, width // spread, rows), jnp.bfloat16)
    return pl.pallas_call(
        functools.partial(gather_kernel, size),
        out_shape=tuple(
            jax.ShapeDtypeStruct((a.shape[0], a.shape[1] * size, a.shape[2]), a.dtype)
            for a in arrays
        )
        + (moved, moved),
        in_specs=[anywhere] * count + [vmem, vmem],
        out_specs=(vmem, vmem) + (anywhere,) * (count - 2) + (anywhere, anywhere),
        scratch_shapes=[
            pltpu.SemaphoreType.DMA((count,)),
            pltpu.SemaphoreType.DMA((count, 3, size)),
            pltpu.SemaphoreType.DMA((count, size)),
            pltpu.VMEM((blocks, width, rows), jnp.bfloat16),
            pltpu.VMEM((blocks, width, rows), jnp.bfloat16),
            pltpu.SemaphoreType.DMA((2,)),
            pltpu.SemaphoreType.DMA((2, spread)),
            pltpu.SemaphoreType.DMA((2, spread)),
        ],
        compiler_params=pltpu.CompilerParams(
            collective_id=0, has_side_effects=True, vmem_limit_bytes=VMEM_BYTES
        ),
        name="gather_rows",
    )(*arrays, tokens, upstream)


class Reduce:
    def __init__(self, place, grad, rows, scale, final, cross, low, high, stage, sems):
        self.p, self.grad, self.rows, self.scale, self.final = place, grad, rows, scale, final
        self.cross, self.low, self.high, self.stage, self.sems = cross, low, high, stage, sems

    def _cross(self, z):
        p = self.p
        return send(
            rows_of(self.grad, p.chunk(z, 1 - p.x), self.rows),
            self.cross.at[z],
            self.sems.at[0, z],
            self.sems.at[1, z],
            p.partner,
        )

    def _up(self, z):
        return send(
            self.stage.at[z], self.low.at[z], self.sems.at[2, z], self.sems.at[3, z],
            self.p.me + SIDE,
        )

    def _down(self, z):
        return send(
            self.stage.at[z], self.high.at[z], self.sems.at[4, z], self.sems.at[5, z],
            self.p.me - SIDE,
        )

    def send_across(self, distance):
        p = self.p
        if distance == 0:
            self._cross(p.z).start()
            return
        pl.when(p.z + distance < p.depth)(lambda: self._cross(p.z + distance).start())
        pl.when(p.z >= distance)(lambda: self._cross(p.z - distance).start())

    def _sum(self, z, others, store):
        first = pl.multiple_of(self.p.chunk(z, self.p.x) * self.rows, self.rows)

        @pl.loop(0, self.grad.shape[0], unroll=2)
        def _(block):
            total = self.grad[block, pl.ds(first, self.rows), :].astype(jnp.float32)
            for other in (self.cross,) + others:
                total = total + other[z, block].astype(jnp.float32)
            store(block, total)

    def step(self, distance):
        p = self.p

        def upward():
            z = p.z + distance
            self._cross(z).wait_recv()

            def store(block, total):
                self.stage[z, block] = total.astype(self.stage.dtype)

            def joined():
                self._up(z).wait_recv()
                self._sum(z, (self.low,), store)

            pl.when(p.has_below())(joined)
            pl.when(jnp.logical_not(p.has_below()))(lambda: self._sum(z, (), store))
            self._up(z).start()

        def downward():
            z = p.z - distance
            self._cross(z).wait_recv()

            def store(block, total):
                self.stage[z, block] = total.astype(self.stage.dtype)

            def joined():
                self._down(z).wait_recv()
                self._sum(z, (self.high,), store)

            pl.when(p.has_above())(joined)
            pl.when(jnp.logical_not(p.has_above()))(lambda: self._sum(z, (), store))
            self._down(z).start()

        pl.when(p.z + distance < p.depth)(upward)
        pl.when(p.z >= distance)(downward)

    def last(self):
        p = self.p

        def store(block, total):
            self.final[block] = (total * self.scale).astype(self.final.dtype)

        self._cross(p.z).wait_recv()
        pl.when(p.has_below())(lambda: self._up(p.z).wait_recv())
        pl.when(p.has_above())(lambda: self._down(p.z).wait_recv())
        low, high = p.has_below(), p.has_above()
        pl.when(jnp.logical_and(low, high))(
            lambda: self._sum(p.z, (self.low, self.high), store)
        )
        pl.when(jnp.logical_not(high))(lambda: self._sum(p.z, (self.low,), store))
        pl.when(jnp.logical_not(low))(lambda: self._sum(p.z, (self.high,), store))

    def finish(self):
        p = self.p
        for z in range(p.depth):
            self._cross(z).wait_send()
        for distance in range(1, p.depth):
            pl.when(p.z + distance < p.depth)(lambda: self._up(p.z + distance).wait_send())
            pl.when(p.z >= distance)(lambda: self._down(p.z - distance).wait_send())


def reduce_kernel(size, scale, *refs):
    count, shared = 4, 2
    grad_us, grad_df, made_down, made_up, tokens, upstream, full_uf = refs[:7]
    input_grad, outs = refs[7], refs[8 : 8 + count]
    grad_ds, grad_uf, moved_down, moved_up = refs[8 + count : 12 + count]
    local_blk, sends_blk, recv_blk = refs[12 + count : 15 + count]
    rest = refs[15 + count :]
    crosses, lows, highs, stages = (rest[k * count : (k + 1) * count] for k in range(4))
    finals = rest[4 * count : 4 * count + shared]
    sems, local, sends, recv = rest[4 * count + shared :]
    grads = (grad_ds, grad_uf, grad_us, grad_df)
    place = Place(size)
    greet(place)
    reduces = [
        Reduce(
            place, grads[a], grads[a].shape[1] // size, scale,
            finals[a] if a < shared else outs[a],
            crosses[a], lows[a], highs[a], stages[a], sems.at[a],
        )
        for a in range(count)
    ]
    gathers = [
        Gather(
            place, finals[a], outs[a], finals[a].shape[1],
            local.at[a], sends.at[a], recv.at[a], False,
        )
        for a in range(shared)
    ]
    down = Exchange(
        made_down, moved_down, local_blk.at[0], sends_blk.at[0], recv_blk.at[0], True
    )
    up = Exchange(made_up, moved_up, local_blk.at[1], sends_blk.at[1], recv_blk.at[1], True)
    blocks, width = grad_uf.shape[0], grad_uf.shape[1]

    def columns_of(block):
        return pl.ds(pl.multiple_of(block * width, width), width)

    def make_ds():
        down.finish()

        @pl.loop(0, blocks, unroll=2)
        def _(block):
            grad_ds[block] = jnp.dot(
                moved_down[block], upstream[:, columns_of(block)],
                preferred_element_type=jnp.float32,
            ).astype(jnp.bfloat16)

        for distance in range(place.depth - 1, -1, -1):
            reduces[0].send_across(distance)

    def make_uf():
        up.finish()

        @pl.loop(0, blocks, unroll=2)
        def _(block):
            product = jnp.dot(
                moved_up[block], tokens[:, columns_of(block)],
                preferred_element_type=jnp.float32,
            )
            grad_uf[block] = product.T.astype(jnp.bfloat16)

        for distance in range(place.depth - 1, -1, -1):
            reduces[1].send_across(distance)

    def make_input_grad():
        @pl.loop(0, blocks, unroll=2)
        def _(block):
            product = jnp.dot(
                full_uf[block], moved_up[block], preferred_element_type=jnp.float32
            )
            input_grad[:, columns_of(block)] = product.T.astype(jnp.bfloat16)

    down.begin()
    up.begin()
    for distance in range(place.depth - 1, -1, -1):
        for reduce in reduces[shared:]:
            reduce.send_across(distance)
    pending = [make_ds, make_uf]
    for distance in range(place.depth - 1, 0, -1):
        for reduce in reduces[shared:]:
            reduce.step(distance)
        if pending:
            pending.pop(0)()
    for make in pending:
        make()
    for distance in range(place.depth - 1, 0, -1):
        for reduce in reduces[:shared]:
            reduce.step(distance)
    for a in range(shared):
        reduces[a].last()
        gathers[a].begin()
    for a in range(shared, count):
        reduces[a].last()
    make_input_grad()
    for distance in range(1, place.depth):
        for gather in gathers:
            gather.step(distance)
    for gather in gathers:
        gather.finish()
    for reduce in reduces:
        reduce.finish()


def reduce_rows(grad_us, grad_df, made_down, made_up, tokens, upstream, full_uf, size, scale):
    depth, spread, shared = size // SIDE, lax.axis_size("blk"), 2
    square = jax.ShapeDtypeStruct(full_uf.shape, jnp.bfloat16)
    grads = (square, square, grad_us, grad_df)
    parts = [(g.shape[0], g.shape[1] // size, g.shape[2]) for g in grads]
    slots = [pltpu.VMEM((depth,) + part, jnp.bfloat16) for part in parts]
    moved = (made_down.shape[0] // spread, made_down.shape[1] * spread, made_down.shape[2])
    vmem = pl.BlockSpec(memory_space=pltpu.VMEM)
    anywhere = pl.BlockSpec(memory_space=pl.ANY)
    count = len(grads)
    return pl.pallas_call(
        functools.partial(reduce_kernel, size, scale),
        out_shape=(jax.ShapeDtypeStruct(tokens.shape, jnp.bfloat16), square, square)
        + tuple(jax.ShapeDtypeStruct(part, jnp.float32) for part in parts[shared:]),
        in_specs=[vmem] * 7,
        out_specs=(vmem, anywhere, anywhere, vmem, vmem),
        scratch_shapes=[pltpu.VMEM(square.shape, jnp.bfloat16)] * 2
        + [pltpu.VMEM(moved, jnp.bfloat16)] * 2
        + [
            pltpu.SemaphoreType.DMA((2,)),
            pltpu.SemaphoreType.DMA((2, spread)),
            pltpu.SemaphoreType.DMA((2, spread)),
        ]
        + slots * 4
        + [pltpu.VMEM(parts[a], jnp.bfloat16) for a in range(shared)]
        + [
            pltpu.SemaphoreType.DMA((count, 6, depth)),
            pltpu.SemaphoreType.DMA((shared,)),
            pltpu.SemaphoreType.DMA((shared, 3, size)),
            pltpu.SemaphoreType.DMA((shared, size)),
        ],
        compiler_params=pltpu.CompilerParams(
            collective_id=1, has_side_effects=True, vmem_limit_bytes=VMEM_BYTES
        ),
        name="reduce_rows",
    )(grad_us, grad_df, made_down, made_up, tokens, upstream, full_uf)


def activation(values):
    return jax.nn.gelu(values, approximate=True)


def permute_forward(lower, second):

    def apply_second(piece):
        if second is None:
            return (piece,)
        product = jnp.einsum("tbj,jbk->tjk", piece, second, preferred_element_type=jnp.float32)
        return (piece, product)

    return apply_second(lax.all_to_all(lower, "blk", split_axis=2, concat_axis=1, tiled=True))


def permute_backward(grad_out, second):
    spread = jnp.einsum(
        "tjk,jbk->tbj", grad_out, second, preferred_element_type=jnp.float32
    ).astype(jnp.bfloat16)
    return lax.all_to_all(spread, "blk", split_axis=1, concat_axis=2, tiled=True)


def by_collectives(tokens, up_first, up_second, down_first, down_second, cotangent):
    tok_rows = tokens.shape[0]
    local_blocks = up_first.shape[0]
    block_size = up_first.shape[2]
    factor = 1.0 / math.sqrt(tok_rows * lax.axis_size("dp"))
    gathered = (
        lax.all_gather(up_first, "dp", axis=1, tiled=True),
        lax.all_gather(up_second, "dp", axis=1, tiled=True),
        lax.all_gather(down_first, "dp", axis=1, tiled=True),
        lax.all_gather(down_second, "dp", axis=1, tiled=True),
    )
    full_uf, full_us, full_df, full_ds = gathered
    inputs_b = tokens.reshape(tok_rows, local_blocks, block_size)
    first_up = jnp.einsum(
        "tbi,bij->tbj", inputs_b, full_uf, preferred_element_type=jnp.float32
    ).astype(jnp.bfloat16)
    moved_up, pre_act = permute_forward(first_up, full_us)
    hidden = activation(pre_act).astype(jnp.bfloat16)
    first_down = jnp.einsum(
        "tbi,bij->tbj", hidden, full_df, preferred_element_type=jnp.float32
    ).astype(jnp.bfloat16)
    moved_down = permute_forward(first_down, None)[0]
    upstream = cotangent.reshape(tok_rows, local_blocks, block_size)
    grad_ds = jnp.einsum("tbj,tjk->jbk", moved_down, upstream, preferred_element_type=jnp.float32)
    back_down = permute_backward(upstream, full_ds)
    grad_df = jnp.einsum("tbi,tbj->bij", hidden, back_down, preferred_element_type=jnp.float32)
    hidden_grad = jnp.einsum("tbj,bij->tbi", back_down, full_df, preferred_element_type=jnp.float32)
    _, pull_back = jax.vjp(activation, pre_act)
    pre_grad = pull_back(hidden_grad)[0].astype(jnp.bfloat16)
    grad_us = jnp.einsum("tbj,tjk->jbk", moved_up, pre_grad, preferred_element_type=jnp.float32)
    back_up = permute_backward(pre_grad, full_us)
    grad_uf = jnp.einsum("tbi,tbj->bij", inputs_b, back_up, preferred_element_type=jnp.float32)
    input_grad = jnp.einsum(
        "tbj,bij->tbi", back_up, full_uf, preferred_element_type=jnp.float32
    ).astype(jnp.bfloat16)
    input_grad = input_grad.reshape(tok_rows, local_blocks * block_size)
    wide_sum = (
        lax.psum_scatter(grad_us, "dp", scatter_dimension=1, tiled=True),
        lax.psum_scatter(grad_df, "dp", scatter_dimension=1, tiled=True),
    )
    square_sum = lax.psum((grad_uf, grad_ds), "dp")
    grad_us = wide_sum[0] * factor
    grad_df = wide_sum[1] * factor
    grad_uf = square_sum[0] * factor
    grad_ds = square_sum[1] * factor
    return (input_grad, grad_uf, grad_us, grad_df, grad_ds)


def per_device(tokens, up_first, up_second, down_first, down_second, cotangent):
    size, spread = lax.axis_size("dp"), lax.axis_size("blk")
    tok_rows = tokens.shape[0]
    local_blocks, _, block_size = up_first.shape
    weights = (down_second, up_first, up_second, down_first)
    tiled = (
        size % SIDE == 0
        and size > SIDE
        and spread > 1
        and all(w.shape[1] % 16 == 0 for w in weights)
        and block_size % (16 * spread) == 0
        and block_size == local_blocks * spread
        and local_blocks % 16 == 0
    )
    if not tiled:
        return by_collectives(tokens, up_first, up_second, down_first, down_second, cotangent)
    factor = 1.0 / math.sqrt(tok_rows * size)
    full_ds, full_uf, full_us, full_df, back_down, moved_up = gather_rows(
        weights, tokens, cotangent, size
    )
    pre_act = jnp.einsum("bjt,jbk->tjk", moved_up, full_us, preferred_element_type=jnp.float32)
    hidden = activation(pre_act).astype(jnp.bfloat16)
    hidden_grad = jnp.einsum("jbt,bij->tbi", back_down, full_df, preferred_element_type=jnp.float32)
    _, pull_back = jax.vjp(activation, pre_act)
    pre_grad = pull_back(hidden_grad)[0].astype(jnp.bfloat16)
    first_down = jnp.einsum(
        "tbi,bij->jbt", hidden, full_df, preferred_element_type=jnp.float32
    ).astype(jnp.bfloat16)
    back_up = jnp.einsum(
        "tjk,jbk->bjt", pre_grad, full_us, preferred_element_type=jnp.float32
    ).astype(jnp.bfloat16)
    grad_df = jnp.einsum("tbi,jbt->bij", hidden, back_down, preferred_element_type=jnp.float32)
    grad_us = jnp.einsum("bjt,tjk->jbk", moved_up, pre_grad, preferred_element_type=jnp.float32)
    input_grad, grad_ds, grad_uf, grad_us, grad_df = reduce_rows(
        grad_us.astype(jnp.bfloat16),
        grad_df.astype(jnp.bfloat16),
        first_down,
        back_up,
        tokens,
        cotangent,
        full_uf,
        size,
        factor,
    )
    return (
        input_grad,
        grad_uf.astype(jnp.float32),
        grad_us,
        grad_df,
        grad_ds.astype(jnp.float32),
    )


def solution(mesh):
    placed = (
        P("dp", "blk"),
        P("blk", "dp", None),
        P("blk", "dp", None),
        P("blk", "dp", None),
        P("blk", "dp", None),
        P("dp", "blk"),
    )
    return jax.shard_map(
        per_device,
        mesh=mesh,
        in_specs=placed,
        out_specs=(
            P("dp", "blk"),
            P("blk", None, None),
            P("blk", "dp", None),
            P("blk", "dp", None),
            P("blk", None, None),
        ),
        check_vma=False,
    )
```

```python
import functools
import math

import jax
import jax.numpy as jnp
from jax import lax
from jax.experimental import pallas as pl
from jax.experimental.pallas import tpu as pltpu
from jax.sharding import PartitionSpec as P

SIDE = 2
VMEM_BYTES = 50 * 1024 * 1024


class Place:
    def __init__(self, size):
        self.depth = size // SIDE
        me = lax.axis_index("dp")
        self.z = lax.div(me, SIDE)
        self.x = lax.rem(me, SIDE)
        self.me = me
        self.partner = self.z * SIDE + (1 - self.x)

    def chunk(self, z, x):
        return z * SIDE + x

    def has_below(self):
        return self.z > 0

    def has_above(self):
        return self.z < self.depth - 1


def greet(place):
    barrier = pltpu.get_barrier_semaphore()

    def tell(target):
        pl.semaphore_signal(
            barrier, inc=1, device_id={"dp": target}, device_id_type=pl.DeviceIdType.MESH
        )

    tell(place.partner)
    pl.when(place.has_below())(lambda: tell(place.me - SIDE))
    pl.when(place.has_above())(lambda: tell(place.me + SIDE))
    spread = lax.axis_size("blk")
    for hop in range(1, spread):
        pl.semaphore_signal(
            barrier,
            inc=1,
            device_id={"blk": lax.rem(lax.axis_index("blk") + hop, spread)},
            device_id_type=pl.DeviceIdType.MESH,
        )
    inner = jnp.logical_and(place.has_below(), place.has_above())
    pl.when(inner)(lambda: pl.semaphore_wait(barrier, spread + 2))
    pl.when(jnp.logical_not(inner))(lambda: pl.semaphore_wait(barrier, spread + 1))


def rows_of(ref, index, rows):
    return ref.at[:, pl.ds(pl.multiple_of(index * rows, rows), rows), :]


def send(src, dst, send_sem, recv_sem, target):
    return pltpu.make_async_remote_copy(
        src_ref=src,
        dst_ref=dst,
        send_sem=send_sem,
        recv_sem=recv_sem,
        device_id={"dp": target},
        device_id_type=pl.DeviceIdType.MESH,
    )


class Gather:
    def __init__(self, place, own, out, rows, local_sem, sends, recv, wide):
        self.p, self.own, self.out, self.rows, self.wide = place, own, out, rows, wide
        self.local_sem, self.sends, self.recv = local_sem, sends, recv

    def _copy(self, index, way, target):
        mine = rows_of(self.out, index, self.rows)
        return send(mine, mine, self.sends.at[way, index], self.recv.at[index], target)

    def _own(self, way, target):
        me = self.p.me
        return send(
            self.own,
            rows_of(self.out, me, self.rows),
            self.sends.at[way, me],
            self.recv.at[me],
            target,
        )

    def _local(self):
        return pltpu.make_async_copy(
            self.own, rows_of(self.out, self.p.me, self.rows), self.local_sem
        )

    def across(self, index):
        return self._copy(index, 0, self.p.partner)

    def up(self, index):
        return self._copy(index, 1, self.p.me + SIDE)

    def down(self, index):
        return self._copy(index, 2, self.p.me - SIDE)

    def begin(self):
        p = self.p
        pl.when(p.has_above())(lambda: self._own(1, p.me + SIDE).start())
        pl.when(p.has_below())(lambda: self._own(2, p.me - SIDE).start())
        self._own(0, p.partner).start()
        self._local().start()

    def landed(self, index):
        self._copy(index, 0, self.p.partner).wait_recv()

    def begin_wide(self):
        p = self.p
        if self.wide:
            self.landed(p.partner)
            pl.when(p.has_above())(lambda: self.up(p.partner).start())
            pl.when(p.has_below())(lambda: self.down(p.partner).start())

    def step(self, distance):
        p = self.p
        columns = (p.x, 1 - p.x) if self.wide else (p.x,)
        for x in columns:

            def from_below():
                index = p.chunk(p.z - distance, x)
                self.landed(index)
                pl.when(p.has_above())(lambda: self.up(index).start())
                if not self.wide:
                    self.across(index).start()

            def from_above():
                index = p.chunk(p.z + distance, x)
                self.landed(index)
                pl.when(p.has_below())(lambda: self.down(index).start())
                if not self.wide:
                    self.across(index).start()

            pl.when(p.z >= distance)(from_below)
            pl.when(p.z + distance < p.depth)(from_above)

    def finish(self):
        p = self.p
        if not self.wide:
            for z in range(p.depth):
                self.landed(p.chunk(z, 1 - p.x))
        self._local().wait()
        self._own(0, p.partner).wait_send()
        columns = (p.x, 1 - p.x) if self.wide else (p.x,)
        for x in columns:
            here = p.chunk(p.z, x)
            pl.when(p.has_above())(lambda: self.up(here).wait_send())
            pl.when(p.has_below())(lambda: self.down(here).wait_send())
            for distance in range(1, p.depth):

                def below():
                    index = p.chunk(p.z - distance, x)
                    pl.when(p.has_above())(lambda: self.up(index).wait_send())
                    if not self.wide:
                        self.across(index).wait_send()

                def above():
                    index = p.chunk(p.z + distance, x)
                    pl.when(p.has_below())(lambda: self.down(index).wait_send())
                    if not self.wide:
                        self.across(index).wait_send()

                pl.when(p.z >= distance)(below)
                pl.when(p.z + distance < p.depth)(above)


class Exchange:
    def __init__(self, made, out, local_sem, sends, recv, leading=False):
        self.leading = leading
        self.made, self.out, self.local_sem, self.sends, self.recv = made, out, local_sem, sends, recv
        self.count = lax.axis_size("blk")
        self.blocks = made.shape[1 if leading else 0]
        self.part = made.shape[0 if leading else 1] // self.count
        self.me = lax.axis_index("blk")

    def _piece(self, target):
        if self.leading:
            return self.made.at[pl.ds(target * self.part, self.part)]
        return rows_of(self.made, target, self.part)

    def _place(self):
        if self.leading:
            return rows_of(self.out, self.me, self.blocks)
        return self.out.at[pl.ds(self.me * self.blocks, self.blocks)]

    def _copy(self, hop):
        target = lax.rem(self.me + hop, self.count)
        return pltpu.make_async_remote_copy(
            src_ref=self._piece(target),
            dst_ref=self._place(),
            send_sem=self.sends.at[hop],
            recv_sem=self.recv.at[hop],
            device_id={"blk": target},
            device_id_type=pl.DeviceIdType.MESH,
        )

    def _local(self):
        return pltpu.make_async_copy(self._piece(self.me), self._place(), self.local_sem)

    def begin(self):
        for hop in range(1, self.count):
            self._copy(hop).start()
        self._local().start()

    def finish(self):
        for hop in range(1, self.count):
            self._copy(hop).wait()
        self._local().wait()


def gather_kernel(size, *refs):
    count = 4
    owns, tokens, upstream = refs[:count], refs[count], refs[count + 1]
    outs, moved_down, moved_up = refs[6 : 6 + count], refs[6 + count], refs[7 + count]
    local, sends, recv, back, first, local_blk, sends_blk, recv_blk = refs[8 + count :]
    place = Place(size)
    greet(place)
    gathers = [
        Gather(
            place, owns[a], outs[a], owns[a].shape[1],
            local.at[a], sends.at[a], recv.at[a], a == 0,
        )
        for a in range(count)
    ]
    down = Exchange(back, moved_down, local_blk.at[0], sends_blk.at[0], recv_blk.at[0])
    up = Exchange(first, moved_up, local_blk.at[1], sends_blk.at[1], recv_blk.at[1])
    blocks, width = first.shape[0], first.shape[1]
    for gather in gathers[:2]:
        gather.begin()
    gathers[0].begin_wide()
    late = list(gathers[2:])
    for distance in range(1, place.depth):
        for gather in gathers[:2]:
            gather.step(distance)
        if late:
            late.pop(0).begin()
    for gather in late:
        gather.begin()
    for gather in gathers[2:]:
        gather.step(1)
    gathers[0].finish()

    @pl.loop(0, blocks, unroll=2)
    def _(block):
        columns = pl.ds(pl.multiple_of(block * width, width), width)
        back[block] = lax.dot_general(
            outs[0][block], upstream[:, columns], (((1,), (1,)), ((), ())),
            preferred_element_type=jnp.float32,
        ).astype(jnp.bfloat16)

    down.begin()
    for distance in range(2, place.depth - 1):
        for gather in gathers[2:]:
            gather.step(distance)
    gathers[1].finish()

    @pl.loop(0, blocks, unroll=2)
    def _(block):
        columns = pl.ds(pl.multiple_of(block * width, width), width)
        product = jnp.dot(
            tokens[:, columns], outs[1][block], preferred_element_type=jnp.float32
        )
        first[block] = product.T.astype(jnp.bfloat16)

    up.begin()
    for gather in gathers[2:]:
        if place.depth > 2:
            gather.step(place.depth - 1)
    for gather in gathers[2:]:
        gather.finish()
    down.finish()
    up.finish()


def gather_rows(arrays, tokens, upstream, size):
    count = len(arrays)
    vmem = pl.BlockSpec(memory_space=pltpu.VMEM)
    anywhere = pl.BlockSpec(memory_space=pl.ANY)
    spread = lax.axis_size("blk")
    blocks, width, rows = arrays[0].shape[0], arrays[0].shape[2], tokens.shape[0]
    moved = jax.ShapeDtypeStruct((blocks * spread, width // spread, rows), jnp.bfloat16)
    return pl.pallas_call(
        functools.partial(gather_kernel, size),
        out_shape=tuple(
            jax.ShapeDtypeStruct((a.shape[0], a.shape[1] * size, a.shape[2]), a.dtype)
            for a in arrays
        )
        + (moved, moved),
        in_specs=[anywhere] * count + [vmem, vmem],
        out_specs=(vmem, vmem) + (anywhere,) * (count - 2) + (anywhere, anywhere),
        scratch_shapes=[
            pltpu.SemaphoreType.DMA((count,)),
            pltpu.SemaphoreType.DMA((count, 3, size)),
            pltpu.SemaphoreType.DMA((count, size)),
            pltpu.VMEM((blocks, width, rows), jnp.bfloat16),
            pltpu.VMEM((blocks, width, rows), jnp.bfloat16),
            pltpu.SemaphoreType.DMA((2,)),
            pltpu.SemaphoreType.DMA((2, spread)),
            pltpu.SemaphoreType.DMA((2, spread)),
        ],
        compiler_params=pltpu.CompilerParams(
            collective_id=0, has_side_effects=True, vmem_limit_bytes=VMEM_BYTES
        ),
        name="gather_rows",
    )(*arrays, tokens, upstream)


class Reduce:
    def __init__(self, place, grad, rows, scale, final, cross, low, high, stage, sems):
        self.p, self.grad, self.rows, self.scale, self.final = place, grad, rows, scale, final
        self.cross, self.low, self.high, self.stage, self.sems = cross, low, high, stage, sems

    def _cross(self, z):
        p = self.p
        return send(
            rows_of(self.grad, p.chunk(z, 1 - p.x), self.rows),
            self.cross.at[z],
            self.sems.at[0, z],
            self.sems.at[1, z],
            p.partner,
        )

    def _up(self, z):
        return send(
            self.stage.at[z], self.low.at[z], self.sems.at[2, z], self.sems.at[3, z],
            self.p.me + SIDE,
        )

    def _down(self, z):
        return send(
            self.stage.at[z], self.high.at[z], self.sems.at[4, z], self.sems.at[5, z],
            self.p.me - SIDE,
        )

    def send_across(self, distance):
        p = self.p
        if distance == 0:
            self._cross(p.z).start()
            return
        pl.when(p.z + distance < p.depth)(lambda: self._cross(p.z + distance).start())
        pl.when(p.z >= distance)(lambda: self._cross(p.z - distance).start())

    def _sum(self, z, others, store):
        first = pl.multiple_of(self.p.chunk(z, self.p.x) * self.rows, self.rows)

        @pl.loop(0, self.grad.shape[0], unroll=2)
        def _(block):
            total = self.grad[block, pl.ds(first, self.rows), :].astype(jnp.float32)
            for other in (self.cross,) + others:
                total = total + other[z, block].astype(jnp.float32)
            store(block, total)

    def step(self, distance):
        p = self.p

        def upward():
            z = p.z + distance
            self._cross(z).wait_recv()

            def store(block, total):
                self.stage[z, block] = total.astype(self.stage.dtype)

            def joined():
                self._up(z).wait_recv()
                self._sum(z, (self.low,), store)

            pl.when(p.has_below())(joined)
            pl.when(jnp.logical_not(p.has_below()))(lambda: self._sum(z, (), store))
            self._up(z).start()

        def downward():
            z = p.z - distance
            self._cross(z).wait_recv()

            def store(block, total):
                self.stage[z, block] = total.astype(self.stage.dtype)

            def joined():
                self._down(z).wait_recv()
                self._sum(z, (self.high,), store)

            pl.when(p.has_above())(joined)
            pl.when(jnp.logical_not(p.has_above()))(lambda: self._sum(z, (), store))
            self._down(z).start()

        pl.when(p.z + distance < p.depth)(upward)
        pl.when(p.z >= distance)(downward)

    def last(self):
        p = self.p

        def store(block, total):
            self.final[block] = (total * self.scale).astype(self.final.dtype)

        self._cross(p.z).wait_recv()
        pl.when(p.has_below())(lambda: self._up(p.z).wait_recv())
        pl.when(p.has_above())(lambda: self._down(p.z).wait_recv())
        low, high = p.has_below(), p.has_above()
        pl.when(jnp.logical_and(low, high))(
            lambda: self._sum(p.z, (self.low, self.high), store)
        )
        pl.when(jnp.logical_not(high))(lambda: self._sum(p.z, (self.low,), store))
        pl.when(jnp.logical_not(low))(lambda: self._sum(p.z, (self.high,), store))

    def finish(self):
        p = self.p
        for z in range(p.depth):
            self._cross(z).wait_send()
        for distance in range(1, p.depth):
            pl.when(p.z + distance < p.depth)(lambda: self._up(p.z + distance).wait_send())
            pl.when(p.z >= distance)(lambda: self._down(p.z - distance).wait_send())


def reduce_kernel(size, scale, *refs):
    count, shared = 4, 2
    grad_us, grad_df, made_down, made_up, tokens, upstream, full_uf = refs[:7]
    input_grad, outs = refs[7], refs[8 : 8 + count]
    grad_ds, grad_uf, moved_down, moved_up = refs[8 + count : 12 + count]
    local_blk, sends_blk, recv_blk = refs[12 + count : 15 + count]
    rest = refs[15 + count :]
    crosses, lows, highs, stages = (rest[k * count : (k + 1) * count] for k in range(4))
    finals = rest[4 * count : 4 * count + shared]
    sems, local, sends, recv = rest[4 * count + shared :]
    grads = (grad_ds, grad_uf, grad_us, grad_df)
    place = Place(size)
    greet(place)
    reduces = [
        Reduce(
            place, grads[a], grads[a].shape[1] // size, scale,
            finals[a] if a < shared else outs[a],
            crosses[a], lows[a], highs[a], stages[a], sems.at[a],
        )
        for a in range(count)
    ]
    gathers = [
        Gather(
            place, finals[a], outs[a], finals[a].shape[1],
            local.at[a], sends.at[a], recv.at[a], a == 0,
        )
        for a in range(shared)
    ]
    down = Exchange(
        made_down, moved_down, local_blk.at[0], sends_blk.at[0], recv_blk.at[0], True
    )
    up = Exchange(made_up, moved_up, local_blk.at[1], sends_blk.at[1], recv_blk.at[1], True)
    blocks, width = grad_uf.shape[0], grad_uf.shape[1]

    def columns_of(block):
        return pl.ds(pl.multiple_of(block * width, width), width)

    def make_ds():
        down.finish()

        @pl.loop(0, blocks, unroll=2)
        def _(block):
            grad_ds[block] = jnp.dot(
                moved_down[block], upstream[:, columns_of(block)],
                preferred_element_type=jnp.float32,
            ).astype(jnp.bfloat16)

        for distance in range(place.depth - 1, -1, -1):
            reduces[0].send_across(distance)

    def make_uf():
        up.finish()

        @pl.loop(0, blocks, unroll=2)
        def _(block):
            product = jnp.dot(
                moved_up[block], tokens[:, columns_of(block)],
                preferred_element_type=jnp.float32,
            )
            grad_uf[block] = product.T.astype(jnp.bfloat16)

        for distance in range(place.depth - 1, -1, -1):
            reduces[1].send_across(distance)

    def make_input_grad():
        @pl.loop(0, blocks, unroll=2)
        def _(block):
            product = jnp.dot(
                full_uf[block], moved_up[block], preferred_element_type=jnp.float32
            )
            input_grad[:, columns_of(block)] = product.T.astype(jnp.bfloat16)

    down.begin()
    up.begin()
    far = range(place.depth - 1, 1, -1)
    for distance in far:
        for reduce in reduces[shared:]:
            reduce.send_across(distance)
    pending = [make_ds, make_uf]
    for distance in far:
        for reduce in reduces[shared:]:
            reduce.step(distance)
        if pending:
            pending.pop(0)()
    for make in pending:
        make()
    for distance in (1, 0):
        for reduce in reduces[shared:]:
            reduce.send_across(distance)
    for distance in range(place.depth - 1, 0, -1):
        for reduce in reduces[:shared]:
            reduce.step(distance)
    for a in range(shared):
        reduces[a].last()
        gathers[a].begin()
    for reduce in reduces[shared:]:
        reduce.step(1)
    gathers[0].begin_wide()
    for gather in gathers:
        gather.step(1)
    for reduce in reduces[shared:]:
        reduce.last()
    for distance in range(2, place.depth):
        for gather in gathers:
            gather.step(distance)
    make_input_grad()
    for gather in gathers:
        gather.finish()
    for reduce in reduces:
        reduce.finish()


def reduce_rows(grad_us, grad_df, made_down, made_up, tokens, upstream, full_uf, size, scale):
    depth, spread, shared = size // SIDE, lax.axis_size("blk"), 2
    square = jax.ShapeDtypeStruct(full_uf.shape, jnp.bfloat16)
    grads = (square, square, grad_us, grad_df)
    parts = [(g.shape[0], g.shape[1] // size, g.shape[2]) for g in grads]
    slots = [pltpu.VMEM((depth,) + part, jnp.bfloat16) for part in parts]
    moved = (made_down.shape[0] // spread, made_down.shape[1] * spread, made_down.shape[2])
    vmem = pl.BlockSpec(memory_space=pltpu.VMEM)
    anywhere = pl.BlockSpec(memory_space=pl.ANY)
    count = len(grads)
    return pl.pallas_call(
        functools.partial(reduce_kernel, size, scale),
        out_shape=(jax.ShapeDtypeStruct(tokens.shape, jnp.bfloat16), square, square)
        + tuple(jax.ShapeDtypeStruct(part, jnp.float32) for part in parts[shared:]),
        in_specs=[vmem] * 7,
        out_specs=(vmem, anywhere, anywhere, vmem, vmem),
        scratch_shapes=[pltpu.VMEM(square.shape, jnp.bfloat16)] * 2
        + [pltpu.VMEM(moved, jnp.bfloat16)] * 2
        + [
            pltpu.SemaphoreType.DMA((2,)),
            pltpu.SemaphoreType.DMA((2, spread)),
            pltpu.SemaphoreType.DMA((2, spread)),
        ]
        + slots * 4
        + [pltpu.VMEM(parts[a], jnp.bfloat16) for a in range(shared)]
        + [
            pltpu.SemaphoreType.DMA((count, 6, depth)),
            pltpu.SemaphoreType.DMA((shared,)),
            pltpu.SemaphoreType.DMA((shared, 3, size)),
            pltpu.SemaphoreType.DMA((shared, size)),
        ],
        compiler_params=pltpu.CompilerParams(
            collective_id=1, has_side_effects=True, vmem_limit_bytes=VMEM_BYTES
        ),
        name="reduce_rows",
    )(grad_us, grad_df, made_down, made_up, tokens, upstream, full_uf)


def activation(values):
    return jax.nn.gelu(values, approximate=True)


def permute_forward(lower, second):

    def apply_second(piece):
        if second is None:
            return (piece,)
        product = jnp.einsum("tbj,jbk->tjk", piece, second, preferred_element_type=jnp.float32)
        return (piece, product)

    return apply_second(lax.all_to_all(lower, "blk", split_axis=2, concat_axis=1, tiled=True))


def permute_backward(grad_out, second):
    spread = jnp.einsum(
        "tjk,jbk->tbj", grad_out, second, preferred_element_type=jnp.float32
    ).astype(jnp.bfloat16)
    return lax.all_to_all(spread, "blk", split_axis=1, concat_axis=2, tiled=True)


def by_collectives(tokens, up_first, up_second, down_first, down_second, cotangent):
    tok_rows = tokens.shape[0]
    local_blocks = up_first.shape[0]
    block_size = up_first.shape[2]
    factor = 1.0 / math.sqrt(tok_rows * lax.axis_size("dp"))
    gathered = (
        lax.all_gather(up_first, "dp", axis=1, tiled=True),
        lax.all_gather(up_second, "dp", axis=1, tiled=True),
        lax.all_gather(down_first, "dp", axis=1, tiled=True),
        lax.all_gather(down_second, "dp", axis=1, tiled=True),
    )
    full_uf, full_us, full_df, full_ds = gathered
    inputs_b = tokens.reshape(tok_rows, local_blocks, block_size)
    first_up = jnp.einsum(
        "tbi,bij->tbj", inputs_b, full_uf, preferred_element_type=jnp.float32
    ).astype(jnp.bfloat16)
    moved_up, pre_act = permute_forward(first_up, full_us)
    hidden = activation(pre_act).astype(jnp.bfloat16)
    first_down = jnp.einsum(
        "tbi,bij->tbj", hidden, full_df, preferred_element_type=jnp.float32
    ).astype(jnp.bfloat16)
    moved_down = permute_forward(first_down, None)[0]
    upstream = cotangent.reshape(tok_rows, local_blocks, block_size)
    grad_ds = jnp.einsum("tbj,tjk->jbk", moved_down, upstream, preferred_element_type=jnp.float32)
    back_down = permute_backward(upstream, full_ds)
    grad_df = jnp.einsum("tbi,tbj->bij", hidden, back_down, preferred_element_type=jnp.float32)
    hidden_grad = jnp.einsum("tbj,bij->tbi", back_down, full_df, preferred_element_type=jnp.float32)
    _, pull_back = jax.vjp(activation, pre_act)
    pre_grad = pull_back(hidden_grad)[0].astype(jnp.bfloat16)
    grad_us = jnp.einsum("tbj,tjk->jbk", moved_up, pre_grad, preferred_element_type=jnp.float32)
    back_up = permute_backward(pre_grad, full_us)
    grad_uf = jnp.einsum("tbi,tbj->bij", inputs_b, back_up, preferred_element_type=jnp.float32)
    input_grad = jnp.einsum(
        "tbj,bij->tbi", back_up, full_uf, preferred_element_type=jnp.float32
    ).astype(jnp.bfloat16)
    input_grad = input_grad.reshape(tok_rows, local_blocks * block_size)
    wide_sum = (
        lax.psum_scatter(grad_us, "dp", scatter_dimension=1, tiled=True),
        lax.psum_scatter(grad_df, "dp", scatter_dimension=1, tiled=True),
    )
    square_sum = lax.psum((grad_uf, grad_ds), "dp")
    grad_us = wide_sum[0] * factor
    grad_df = wide_sum[1] * factor
    grad_uf = square_sum[0] * factor
    grad_ds = square_sum[1] * factor
    return (input_grad, grad_uf, grad_us, grad_df, grad_ds)


def per_device(tokens, up_first, up_second, down_first, down_second, cotangent):
    size, spread = lax.axis_size("dp"), lax.axis_size("blk")
    tok_rows = tokens.shape[0]
    local_blocks, _, block_size = up_first.shape
    weights = (down_second, up_first, up_second, down_first)
    tiled = (
        size % SIDE == 0
        and size > SIDE
        and spread > 1
        and all(w.shape[1] % 16 == 0 for w in weights)
        and block_size % (16 * spread) == 0
        and block_size == local_blocks * spread
        and local_blocks % 16 == 0
    )
    if not tiled:
        return by_collectives(tokens, up_first, up_second, down_first, down_second, cotangent)
    factor = 1.0 / math.sqrt(tok_rows * size)
    full_ds, full_uf, full_us, full_df, back_down, moved_up = gather_rows(
        weights, tokens, cotangent, size
    )
    pre_act = jnp.einsum("bjt,jbk->tjk", moved_up, full_us, preferred_element_type=jnp.float32)
    hidden = activation(pre_act).astype(jnp.bfloat16)
    hidden_grad = jnp.einsum("jbt,bij->tbi", back_down, full_df, preferred_element_type=jnp.float32)
    _, pull_back = jax.vjp(activation, pre_act)
    pre_grad = pull_back(hidden_grad)[0].astype(jnp.bfloat16)
    first_down = jnp.einsum(
        "tbi,bij->jbt", hidden, full_df, preferred_element_type=jnp.float32
    ).astype(jnp.bfloat16)
    back_up = jnp.einsum(
        "tjk,jbk->bjt", pre_grad, full_us, preferred_element_type=jnp.float32
    ).astype(jnp.bfloat16)
    grad_df = jnp.einsum("tbi,jbt->bij", hidden, back_down, preferred_element_type=jnp.float32)
    grad_us = jnp.einsum("bjt,tjk->jbk", moved_up, pre_grad, preferred_element_type=jnp.float32)
    input_grad, grad_ds, grad_uf, grad_us, grad_df = reduce_rows(
        grad_us.astype(jnp.bfloat16),
        grad_df.astype(jnp.bfloat16),
        first_down,
        back_up,
        tokens,
        cotangent,
        full_uf,
        size,
        factor,
    )
    return (
        input_grad,
        grad_uf.astype(jnp.float32),
        grad_us,
        grad_df,
        grad_ds.astype(jnp.float32),
    )


def solution(mesh):
    placed = (
        P("dp", "blk"),
        P("blk", "dp", None),
        P("blk", "dp", None),
        P("blk", "dp", None),
        P("blk", "dp", None),
        P("dp", "blk"),
    )
    return jax.shard_map(
        per_device,
        mesh=mesh,
        in_specs=placed,
        out_specs=(
            P("dp", "blk"),
            P("blk", None, None),
            P("blk", "dp", None),
            P("blk", "dp", None),
            P("blk", None, None),
        ),
        check_vma=False,
    )
```

```python
import functools
import math

import jax
import jax.numpy as jnp
from jax import lax
from jax.experimental import pallas as pl
from jax.experimental.pallas import tpu as pltpu
from jax.sharding import PartitionSpec as P

SIDE = 2
VMEM_BYTES = 50 * 1024 * 1024


class Place:
    def __init__(self, size):
        self.depth = size // SIDE
        me = lax.axis_index("dp")
        self.z = lax.div(me, SIDE)
        self.x = lax.rem(me, SIDE)
        self.me = me
        self.partner = self.z * SIDE + (1 - self.x)

    def chunk(self, z, x):
        return z * SIDE + x

    def has_below(self):
        return self.z > 0

    def has_above(self):
        return self.z < self.depth - 1


def greet(place):
    barrier = pltpu.get_barrier_semaphore()

    def tell(target):
        pl.semaphore_signal(
            barrier, inc=1, device_id={"dp": target}, device_id_type=pl.DeviceIdType.MESH
        )

    tell(place.partner)
    pl.when(place.has_below())(lambda: tell(place.me - SIDE))
    pl.when(place.has_above())(lambda: tell(place.me + SIDE))
    spread = lax.axis_size("blk")
    for hop in range(1, spread):
        pl.semaphore_signal(
            barrier,
            inc=1,
            device_id={"blk": lax.rem(lax.axis_index("blk") + hop, spread)},
            device_id_type=pl.DeviceIdType.MESH,
        )
    inner = jnp.logical_and(place.has_below(), place.has_above())
    pl.when(inner)(lambda: pl.semaphore_wait(barrier, spread + 2))
    pl.when(jnp.logical_not(inner))(lambda: pl.semaphore_wait(barrier, spread + 1))


def rows_of(ref, index, rows):
    return ref.at[:, pl.ds(pl.multiple_of(index * rows, rows), rows), :]


def send(src, dst, send_sem, recv_sem, target):
    return pltpu.make_async_remote_copy(
        src_ref=src,
        dst_ref=dst,
        send_sem=send_sem,
        recv_sem=recv_sem,
        device_id={"dp": target},
        device_id_type=pl.DeviceIdType.MESH,
    )


class Gather:
    def __init__(self, place, own, out, rows, local_sem, sends, recv, wide):
        self.p, self.own, self.out, self.rows, self.wide = place, own, out, rows, wide
        self.local_sem, self.sends, self.recv = local_sem, sends, recv

    def _copy(self, index, way, target):
        mine = rows_of(self.out, index, self.rows)
        return send(mine, mine, self.sends.at[way, index], self.recv.at[index], target)

    def _own(self, way, target):
        me = self.p.me
        return send(
            self.own,
            rows_of(self.out, me, self.rows),
            self.sends.at[way, me],
            self.recv.at[me],
            target,
        )

    def _local(self):
        return pltpu.make_async_copy(
            self.own, rows_of(self.out, self.p.me, self.rows), self.local_sem
        )

    def across(self, index):
        return self._copy(index, 0, self.p.partner)

    def up(self, index):
        return self._copy(index, 1, self.p.me + SIDE)

    def down(self, index):
        return self._copy(index, 2, self.p.me - SIDE)

    def begin(self):
        p = self.p
        pl.when(p.has_above())(lambda: self._own(1, p.me + SIDE).start())
        pl.when(p.has_below())(lambda: self._own(2, p.me - SIDE).start())
        self._own(0, p.partner).start()
        self._local().start()

    def landed(self, index):
        self._copy(index, 0, self.p.partner).wait_recv()

    def begin_wide(self):
        p = self.p
        if self.wide:
            self.landed(p.partner)
            pl.when(p.has_above())(lambda: self.up(p.partner).start())
            pl.when(p.has_below())(lambda: self.down(p.partner).start())

    def step(self, distance):
        p = self.p
        columns = (p.x, 1 - p.x) if self.wide else (p.x,)
        for x in columns:

            def from_below():
                index = p.chunk(p.z - distance, x)
                self.landed(index)
                pl.when(p.has_above())(lambda: self.up(index).start())
                if not self.wide:
                    self.across(index).start()

            def from_above():
                index = p.chunk(p.z + distance, x)
                self.landed(index)
                pl.when(p.has_below())(lambda: self.down(index).start())
                if not self.wide:
                    self.across(index).start()

            pl.when(p.z >= distance)(from_below)
            pl.when(p.z + distance < p.depth)(from_above)

    def finish(self):
        p = self.p
        if not self.wide:
            for z in range(p.depth):
                self.landed(p.chunk(z, 1 - p.x))
        self._local().wait()
        self._own(0, p.partner).wait_send()
        columns = (p.x, 1 - p.x) if self.wide else (p.x,)
        for x in columns:
            here = p.chunk(p.z, x)
            pl.when(p.has_above())(lambda: self.up(here).wait_send())
            pl.when(p.has_below())(lambda: self.down(here).wait_send())
            for distance in range(1, p.depth):

                def below():
                    index = p.chunk(p.z - distance, x)
                    pl.when(p.has_above())(lambda: self.up(index).wait_send())
                    if not self.wide:
                        self.across(index).wait_send()

                def above():
                    index = p.chunk(p.z + distance, x)
                    pl.when(p.has_below())(lambda: self.down(index).wait_send())
                    if not self.wide:
                        self.across(index).wait_send()

                pl.when(p.z >= distance)(below)
                pl.when(p.z + distance < p.depth)(above)


class Exchange:
    def __init__(self, made, out, local_sem, sends, recv, leading=False):
        self.leading = leading
        self.made, self.out, self.local_sem, self.sends, self.recv = made, out, local_sem, sends, recv
        self.count = lax.axis_size("blk")
        self.blocks = made.shape[1 if leading else 0]
        self.part = made.shape[0 if leading else 1] // self.count
        self.me = lax.axis_index("blk")

    def _piece(self, target):
        if self.leading:
            return self.made.at[pl.ds(target * self.part, self.part)]
        return rows_of(self.made, target, self.part)

    def _place(self):
        if self.leading:
            return rows_of(self.out, self.me, self.blocks)
        return self.out.at[pl.ds(self.me * self.blocks, self.blocks)]

    def _copy(self, hop):
        target = lax.rem(self.me + hop, self.count)
        return pltpu.make_async_remote_copy(
            src_ref=self._piece(target),
            dst_ref=self._place(),
            send_sem=self.sends.at[hop],
            recv_sem=self.recv.at[hop],
            device_id={"blk": target},
            device_id_type=pl.DeviceIdType.MESH,
        )

    def _local(self):
        return pltpu.make_async_copy(self._piece(self.me), self._place(), self.local_sem)

    def begin(self):
        for hop in range(1, self.count):
            self._copy(hop).start()
        self._local().start()

    def finish(self):
        for hop in range(1, self.count):
            self._copy(hop).wait()
        self._local().wait()


def gather_kernel(size, *refs):
    count = 4
    owns, tokens, upstream = refs[:count], refs[count], refs[count + 1]
    outs, moved_down, moved_up = refs[6 : 6 + count], refs[6 + count], refs[7 + count]
    local, sends, recv, back, first, local_blk, sends_blk, recv_blk = refs[8 + count :]
    place = Place(size)
    greet(place)
    gathers = [
        Gather(
            place, owns[a], outs[a], owns[a].shape[1],
            local.at[a], sends.at[a], recv.at[a], a == 0,
        )
        for a in range(count)
    ]
    down = Exchange(back, moved_down, local_blk.at[0], sends_blk.at[0], recv_blk.at[0])
    up = Exchange(first, moved_up, local_blk.at[1], sends_blk.at[1], recv_blk.at[1])
    blocks, width = first.shape[0], first.shape[1]
    for gather in gathers[:2]:
        gather.begin()
    gathers[0].begin_wide()
    late = list(gathers[2:])
    for distance in range(1, place.depth):
        for gather in gathers[:2]:
            gather.step(distance)
        if late:
            late.pop(0).begin()
    for gather in late:
        gather.begin()
    for gather in gathers[2:]:
        gather.step(1)
    gathers[0].finish()

    @pl.loop(0, blocks, unroll=2)
    def _(block):
        columns = pl.ds(pl.multiple_of(block * width, width), width)
        back[block] = lax.dot_general(
            outs[0][block], upstream[:, columns], (((1,), (1,)), ((), ())),
            preferred_element_type=jnp.float32,
        ).astype(jnp.bfloat16)

    down.begin()
    for distance in range(2, place.depth - 1):
        for gather in gathers[2:]:
            gather.step(distance)
    gathers[1].finish()

    @pl.loop(0, blocks, unroll=2)
    def _(block):
        columns = pl.ds(pl.multiple_of(block * width, width), width)
        product = jnp.dot(
            tokens[:, columns], outs[1][block], preferred_element_type=jnp.float32
        )
        first[block] = product.T.astype(jnp.bfloat16)

    up.begin()
    for gather in gathers[2:]:
        if place.depth > 2:
            gather.step(place.depth - 1)
    for gather in gathers[2:]:
        gather.finish()
    down.finish()
    up.finish()


def gather_rows(arrays, tokens, upstream, size):
    count = len(arrays)
    vmem = pl.BlockSpec(memory_space=pltpu.VMEM)
    anywhere = pl.BlockSpec(memory_space=pl.ANY)
    spread = lax.axis_size("blk")
    blocks, width, rows = arrays[0].shape[0], arrays[0].shape[2], tokens.shape[0]
    moved = jax.ShapeDtypeStruct((blocks * spread, width // spread, rows), jnp.bfloat16)
    return pl.pallas_call(
        functools.partial(gather_kernel, size),
        out_shape=tuple(
            jax.ShapeDtypeStruct((a.shape[0], a.shape[1] * size, a.shape[2]), a.dtype)
            for a in arrays
        )
        + (moved, moved),
        in_specs=[anywhere] * count + [vmem, vmem],
        out_specs=(vmem, vmem) + (anywhere,) * (count - 2) + (anywhere, anywhere),
        scratch_shapes=[
            pltpu.SemaphoreType.DMA((count,)),
            pltpu.SemaphoreType.DMA((count, 3, size)),
            pltpu.SemaphoreType.DMA((count, size)),
            pltpu.VMEM((blocks, width, rows), jnp.bfloat16),
            pltpu.VMEM((blocks, width, rows), jnp.bfloat16),
            pltpu.SemaphoreType.DMA((2,)),
            pltpu.SemaphoreType.DMA((2, spread)),
            pltpu.SemaphoreType.DMA((2, spread)),
        ],
        compiler_params=pltpu.CompilerParams(
            collective_id=0, has_side_effects=True, vmem_limit_bytes=VMEM_BYTES
        ),
        name="gather_rows",
    )(*arrays, tokens, upstream)


class Reduce:
    def __init__(self, place, grad, rows, scale, final, cross, low, high, stage, sems):
        self.p, self.grad, self.rows, self.scale, self.final = place, grad, rows, scale, final
        self.cross, self.low, self.high, self.stage, self.sems = cross, low, high, stage, sems

    def _cross(self, z):
        p = self.p
        return send(
            rows_of(self.grad, p.chunk(z, 1 - p.x), self.rows),
            self.cross.at[z],
            self.sems.at[0, z],
            self.sems.at[1, z],
            p.partner,
        )

    def _up(self, z):
        return send(
            self.stage.at[z], self.low.at[z], self.sems.at[2, z], self.sems.at[3, z],
            self.p.me + SIDE,
        )

    def _down(self, z):
        return send(
            self.stage.at[z], self.high.at[z], self.sems.at[4, z], self.sems.at[5, z],
            self.p.me - SIDE,
        )

    def send_across(self, distance):
        p = self.p
        if distance == 0:
            self._cross(p.z).start()
            return
        pl.when(p.z + distance < p.depth)(lambda: self._cross(p.z + distance).start())
        pl.when(p.z >= distance)(lambda: self._cross(p.z - distance).start())

    def _sum(self, z, others, store):
        first = pl.multiple_of(self.p.chunk(z, self.p.x) * self.rows, self.rows)

        @pl.loop(0, self.grad.shape[0], unroll=2)
        def _(block):
            total = self.grad[block, pl.ds(first, self.rows), :].astype(jnp.float32)
            for other in (self.cross,) + others:
                total = total + other[z, block].astype(jnp.float32)
            store(block, total)

    def step(self, distance):
        p = self.p

        def upward():
            z = p.z + distance
            self._cross(z).wait_recv()

            def store(block, total):
                self.stage[z, block] = total.astype(self.stage.dtype)

            def joined():
                self._up(z).wait_recv()
                self._sum(z, (self.low,), store)

            pl.when(p.has_below())(joined)
            pl.when(jnp.logical_not(p.has_below()))(lambda: self._sum(z, (), store))
            self._up(z).start()

        def downward():
            z = p.z - distance
            self._cross(z).wait_recv()

            def store(block, total):
                self.stage[z, block] = total.astype(self.stage.dtype)

            def joined():
                self._down(z).wait_recv()
                self._sum(z, (self.high,), store)

            pl.when(p.has_above())(joined)
            pl.when(jnp.logical_not(p.has_above()))(lambda: self._sum(z, (), store))
            self._down(z).start()

        pl.when(p.z + distance < p.depth)(upward)
        pl.when(p.z >= distance)(downward)

    def last(self):
        p = self.p

        def store(block, total):
            self.final[block] = (total * self.scale).astype(self.final.dtype)

        self._cross(p.z).wait_recv()
        pl.when(p.has_below())(lambda: self._up(p.z).wait_recv())
        pl.when(p.has_above())(lambda: self._down(p.z).wait_recv())
        low, high = p.has_below(), p.has_above()
        pl.when(jnp.logical_and(low, high))(
            lambda: self._sum(p.z, (self.low, self.high), store)
        )
        pl.when(jnp.logical_not(high))(lambda: self._sum(p.z, (self.low,), store))
        pl.when(jnp.logical_not(low))(lambda: self._sum(p.z, (self.high,), store))

    def finish(self):
        p = self.p
        for z in range(p.depth):
            self._cross(z).wait_send()
        for distance in range(1, p.depth):
            pl.when(p.z + distance < p.depth)(lambda: self._up(p.z + distance).wait_send())
            pl.when(p.z >= distance)(lambda: self._down(p.z - distance).wait_send())


def reduce_kernel(size, scale, *refs):
    count, shared = 4, 2
    grad_us, grad_df, made_down, made_up, tokens, upstream, full_uf = refs[:7]
    input_grad, outs = refs[7], refs[8 : 8 + count]
    grad_ds, grad_uf, moved_down, moved_up = refs[8 + count : 12 + count]
    local_blk, sends_blk, recv_blk = refs[12 + count : 15 + count]
    rest = refs[15 + count :]
    crosses, lows, highs, stages = (rest[k * count : (k + 1) * count] for k in range(4))
    finals = rest[4 * count : 4 * count + shared]
    sems, local, sends, recv = rest[4 * count + shared :]
    grads = (grad_ds, grad_uf, grad_us, grad_df)
    place = Place(size)
    greet(place)
    reduces = [
        Reduce(
            place, grads[a], grads[a].shape[1] // size, scale,
            finals[a] if a < shared else outs[a],
            crosses[a], lows[a], highs[a], stages[a], sems.at[a],
        )
        for a in range(count)
    ]
    gathers = [
        Gather(
            place, finals[a], outs[a], finals[a].shape[1],
            local.at[a], sends.at[a], recv.at[a], a == 0,
        )
        for a in range(shared)
    ]
    down = Exchange(
        made_down, moved_down, local_blk.at[0], sends_blk.at[0], recv_blk.at[0], True
    )
    up = Exchange(made_up, moved_up, local_blk.at[1], sends_blk.at[1], recv_blk.at[1], True)
    blocks, width = grad_uf.shape[0], grad_uf.shape[1]

    def columns_of(block):
        return pl.ds(pl.multiple_of(block * width, width), width)

    def make_ds():
        down.finish()

        @pl.loop(0, blocks, unroll=2)
        def _(block):
            grad_ds[block] = jnp.dot(
                moved_down[block], upstream[:, columns_of(block)],
                preferred_element_type=jnp.float32,
            ).astype(jnp.bfloat16)

        for distance in range(place.depth - 1, -1, -1):
            reduces[0].send_across(distance)

    def make_uf():
        up.finish()

        @pl.loop(0, blocks, unroll=2)
        def _(block):
            product = jnp.dot(
                moved_up[block], tokens[:, columns_of(block)],
                preferred_element_type=jnp.float32,
            )
            grad_uf[block] = product.T.astype(jnp.bfloat16)

        for distance in range(place.depth - 1, -1, -1):
            reduces[1].send_across(distance)

    def make_input_grad():
        @pl.loop(0, blocks, unroll=2)
        def _(block):
            product = jnp.dot(
                full_uf[block], moved_up[block], preferred_element_type=jnp.float32
            )
            input_grad[:, columns_of(block)] = product.T.astype(jnp.bfloat16)

    down.begin()
    up.begin()
    far = range(place.depth - 1, 1, -1)
    for distance in range(place.depth - 1, 0, -1):
        for reduce in reduces[shared:]:
            reduce.send_across(distance)
    pending = [make_ds, make_uf]
    for distance in far:
        for reduce in reduces[shared:]:
            reduce.step(distance)
        if pending:
            pending.pop(0)()
    for make in pending:
        make()
    for reduce in reduces[shared:]:
        reduce.send_across(0)
    for reduce in reduces[shared:]:
        reduce.step(1)
    for distance in range(place.depth - 1, 0, -1):
        for reduce in reduces[:shared]:
            reduce.step(distance)
    for a in range(shared):
        reduces[a].last()
        gathers[a].begin()
    gathers[0].begin_wide()
    for gather in gathers:
        gather.step(1)
    for reduce in reduces[shared:]:
        reduce.last()
    for distance in range(2, place.depth):
        for gather in gathers:
            gather.step(distance)
    make_input_grad()
    for gather in gathers:
        gather.finish()
    for reduce in reduces:
        reduce.finish()


def reduce_rows(grad_us, grad_df, made_down, made_up, tokens, upstream, full_uf, size, scale):
    depth, spread, shared = size // SIDE, lax.axis_size("blk"), 2
    square = jax.ShapeDtypeStruct(full_uf.shape, jnp.bfloat16)
    grads = (square, square, grad_us, grad_df)
    parts = [(g.shape[0], g.shape[1] // size, g.shape[2]) for g in grads]
    slots = [pltpu.VMEM((depth,) + part, jnp.bfloat16) for part in parts]
    moved = (made_down.shape[0] // spread, made_down.shape[1] * spread, made_down.shape[2])
    vmem = pl.BlockSpec(memory_space=pltpu.VMEM)
    anywhere = pl.BlockSpec(memory_space=pl.ANY)
    count = len(grads)
    return pl.pallas_call(
        functools.partial(reduce_kernel, size, scale),
        out_shape=(jax.ShapeDtypeStruct(tokens.shape, jnp.bfloat16), square, square)
        + tuple(jax.ShapeDtypeStruct(part, jnp.float32) for part in parts[shared:]),
        in_specs=[vmem] * 7,
        out_specs=(vmem, anywhere, anywhere, vmem, vmem),
        scratch_shapes=[pltpu.VMEM(square.shape, jnp.bfloat16)] * 2
        + [pltpu.VMEM(moved, jnp.bfloat16)] * 2
        + [
            pltpu.SemaphoreType.DMA((2,)),
            pltpu.SemaphoreType.DMA((2, spread)),
            pltpu.SemaphoreType.DMA((2, spread)),
        ]
        + slots * 4
        + [pltpu.VMEM(parts[a], jnp.bfloat16) for a in range(shared)]
        + [
            pltpu.SemaphoreType.DMA((count, 6, depth)),
            pltpu.SemaphoreType.DMA((shared,)),
            pltpu.SemaphoreType.DMA((shared, 3, size)),
            pltpu.SemaphoreType.DMA((shared, size)),
        ],
        compiler_params=pltpu.CompilerParams(
            collective_id=1, has_side_effects=True, vmem_limit_bytes=VMEM_BYTES
        ),
        name="reduce_rows",
    )(grad_us, grad_df, made_down, made_up, tokens, upstream, full_uf)


def activation(values):
    return jax.nn.gelu(values, approximate=True)


def permute_forward(lower, second):

    def apply_second(piece):
        if second is None:
            return (piece,)
        product = jnp.einsum("tbj,jbk->tjk", piece, second, preferred_element_type=jnp.float32)
        return (piece, product)

    return apply_second(lax.all_to_all(lower, "blk", split_axis=2, concat_axis=1, tiled=True))


def permute_backward(grad_out, second):
    spread = jnp.einsum(
        "tjk,jbk->tbj", grad_out, second, preferred_element_type=jnp.float32
    ).astype(jnp.bfloat16)
    return lax.all_to_all(spread, "blk", split_axis=1, concat_axis=2, tiled=True)


def by_collectives(tokens, up_first, up_second, down_first, down_second, cotangent):
    tok_rows = tokens.shape[0]
    local_blocks = up_first.shape[0]
    block_size = up_first.shape[2]
    factor = 1.0 / math.sqrt(tok_rows * lax.axis_size("dp"))
    gathered = (
        lax.all_gather(up_first, "dp", axis=1, tiled=True),
        lax.all_gather(up_second, "dp", axis=1, tiled=True),
        lax.all_gather(down_first, "dp", axis=1, tiled=True),
        lax.all_gather(down_second, "dp", axis=1, tiled=True),
    )
    full_uf, full_us, full_df, full_ds = gathered
    inputs_b = tokens.reshape(tok_rows, local_blocks, block_size)
    first_up = jnp.einsum(
        "tbi,bij->tbj", inputs_b, full_uf, preferred_element_type=jnp.float32
    ).astype(jnp.bfloat16)
    moved_up, pre_act = permute_forward(first_up, full_us)
    hidden = activation(pre_act).astype(jnp.bfloat16)
    first_down = jnp.einsum(
        "tbi,bij->tbj", hidden, full_df, preferred_element_type=jnp.float32
    ).astype(jnp.bfloat16)
    moved_down = permute_forward(first_down, None)[0]
    upstream = cotangent.reshape(tok_rows, local_blocks, block_size)
    grad_ds = jnp.einsum("tbj,tjk->jbk", moved_down, upstream, preferred_element_type=jnp.float32)
    back_down = permute_backward(upstream, full_ds)
    grad_df = jnp.einsum("tbi,tbj->bij", hidden, back_down, preferred_element_type=jnp.float32)
    hidden_grad = jnp.einsum("tbj,bij->tbi", back_down, full_df, preferred_element_type=jnp.float32)
    _, pull_back = jax.vjp(activation, pre_act)
    pre_grad = pull_back(hidden_grad)[0].astype(jnp.bfloat16)
    grad_us = jnp.einsum("tbj,tjk->jbk", moved_up, pre_grad, preferred_element_type=jnp.float32)
    back_up = permute_backward(pre_grad, full_us)
    grad_uf = jnp.einsum("tbi,tbj->bij", inputs_b, back_up, preferred_element_type=jnp.float32)
    input_grad = jnp.einsum(
        "tbj,bij->tbi", back_up, full_uf, preferred_element_type=jnp.float32
    ).astype(jnp.bfloat16)
    input_grad = input_grad.reshape(tok_rows, local_blocks * block_size)
    wide_sum = (
        lax.psum_scatter(grad_us, "dp", scatter_dimension=1, tiled=True),
        lax.psum_scatter(grad_df, "dp", scatter_dimension=1, tiled=True),
    )
    square_sum = lax.psum((grad_uf, grad_ds), "dp")
    grad_us = wide_sum[0] * factor
    grad_df = wide_sum[1] * factor
    grad_uf = square_sum[0] * factor
    grad_ds = square_sum[1] * factor
    return (input_grad, grad_uf, grad_us, grad_df, grad_ds)


def per_device(tokens, up_first, up_second, down_first, down_second, cotangent):
    size, spread = lax.axis_size("dp"), lax.axis_size("blk")
    tok_rows = tokens.shape[0]
    local_blocks, _, block_size = up_first.shape
    weights = (down_second, up_first, up_second, down_first)
    tiled = (
        size % SIDE == 0
        and size > SIDE
        and spread > 1
        and all(w.shape[1] % 16 == 0 for w in weights)
        and block_size % (16 * spread) == 0
        and block_size == local_blocks * spread
        and local_blocks % 16 == 0
    )
    if not tiled:
        return by_collectives(tokens, up_first, up_second, down_first, down_second, cotangent)
    factor = 1.0 / math.sqrt(tok_rows * size)
    full_ds, full_uf, full_us, full_df, back_down, moved_up = gather_rows(
        weights, tokens, cotangent, size
    )
    pre_act = jnp.einsum("bjt,jbk->tjk", moved_up, full_us, preferred_element_type=jnp.float32)
    hidden = activation(pre_act).astype(jnp.bfloat16)
    hidden_grad = jnp.einsum("jbt,bij->tbi", back_down, full_df, preferred_element_type=jnp.float32)
    _, pull_back = jax.vjp(activation, pre_act)
    pre_grad = pull_back(hidden_grad)[0].astype(jnp.bfloat16)
    first_down = jnp.einsum(
        "tbi,bij->jbt", hidden, full_df, preferred_element_type=jnp.float32
    ).astype(jnp.bfloat16)
    back_up = jnp.einsum(
        "tjk,jbk->bjt", pre_grad, full_us, preferred_element_type=jnp.float32
    ).astype(jnp.bfloat16)
    grad_df = jnp.einsum("tbi,jbt->bij", hidden, back_down, preferred_element_type=jnp.float32)
    grad_us = jnp.einsum("bjt,tjk->jbk", moved_up, pre_grad, preferred_element_type=jnp.float32)
    input_grad, grad_ds, grad_uf, grad_us, grad_df = reduce_rows(
        grad_us.astype(jnp.bfloat16),
        grad_df.astype(jnp.bfloat16),
        first_down,
        back_up,
        tokens,
        cotangent,
        full_uf,
        size,
        factor,
    )
    return (
        input_grad,
        grad_uf.astype(jnp.float32),
        grad_us,
        grad_df,
        grad_ds.astype(jnp.float32),
    )


def solution(mesh):
    placed = (
        P("dp", "blk"),
        P("blk", "dp", None),
        P("blk", "dp", None),
        P("blk", "dp", None),
        P("blk", "dp", None),
        P("dp", "blk"),
    )
    return jax.shard_map(
        per_device,
        mesh=mesh,
        in_specs=placed,
        out_specs=(
            P("dp", "blk"),
            P("blk", None, None),
            P("blk", "dp", None),
            P("blk", "dp", None),
            P("blk", None, None),
        ),
        check_vma=False,
    )
```
